512 devices in a mesh: node: 64 (over y, x, z_lo), rel: 8 (over z_hi, core).
Axes of the slice: x: 4, y: 4, z: 16 (z_hi: 4, z_lo: 4; z = z_hi * 4 + z_lo), core: 2. Of those that a mesh axis runs over, the one named last changes fastest.
Arguments:
- features: bfloat16 [8, 1024, 768], P('rel', 'node'), may hold values from -6 to 6
- bases: bfloat16 [30, 768, 1024], P(None, 'node', 'rel'), may hold values from -0.21875 to 0.21875
- coefficients: float32 [6, 30], replicated, may hold values from -0.4375 to 0.4375
- tile_values: bfloat16 [64, 8, 56, 128, 128], P('node', 'rel'), may hold values from -0.03125 to 0.03125
- tile_source: int32 [64, 8, 56], P('node', 'rel'), may hold values from 0 to 7
- tile_relation: int32 [64, 8, 56], P('node', 'rel'), may hold values from 0 to 4
- tile_count: int32 [64, 8], P('node', 'rel'), may hold values from 14 to 56, as said below
Outputs:
- layer_output: bfloat16 [8, 1024, 1024], P('rel', 'node')
The draws below stay inside these ranges and needn't reach their ends.
Inputs may be any that keep to these rules, and one draw needn't show every extreme that they name: `tile_count`: the live slots of each stretch and group are its first ones; in every draw some stretch and group has all 56 slots live.
All inputs are finite; a program needn't handle non-finite values.
Results may differ from the reference program's by a relative error of at most 0.0054.
Values may be sent and summed in bfloat16 or wider, within the bound.
No kernel may reach another device: no remote copies, remote signals or barrier semaphores. Data moves between devices by JAX's collectives and lax.ppermute only.
A program may use at most 64 MiB of HBM per device.

```python
import jax
import jax.numpy as jnp
from jax import lax

DIN = 768
DOUT = 1024
NBASES = 30
RELS = 5
TILE = 128
ROWS = 16
SLOTS = 56
GROUPS = 8
STRETCHES = 64
DEST = 128
GROUP_ROWS = 1024
SRC_BLOCKS = 8


def draw_tile_count(key, part):
    first_key = jax.random.fold_in(key, 11)
    second_key = jax.random.fold_in(key, 12)
    third_key = jax.random.fold_in(key, 13)
    base_count = jax.random.randint(first_key, (STRETCHES, GROUPS), SLOTS // 4, SLOTS // 2 + 1)
    full_mask = jax.random.randint(second_key, (STRETCHES, GROUPS), 0, 8) == 0
    chosen = jax.random.randint(third_key, (), 0, STRETCHES * GROUPS)
    forced = jnp.arange(STRETCHES * GROUPS, dtype=jnp.int32).reshape(STRETCHES, GROUPS) == chosen
    return jnp.where(full_mask | forced, SLOTS, base_count).astype(jnp.int32)


def touch_ends(entries, rng, least, largest):
    longest = entries.shape.index(max(entries.shape))
    spots = []
    for shift in (0, 1):
        where = [jax.random.randint(jax.random.fold_in(rng, axis), (), 0, length) for axis, length in enumerate(entries.shape)]
        where[longest] = (where[longest] + shift) % entries.shape[longest]
        spots.append(tuple(where))
    return entries.at[spots[0]].set(least).at[spots[1]].set(largest)


def level_of(key, dims, shards, smallest, high):
    def one(axis_at, parts):
        steps = jax.random.uniform(jax.random.fold_in(jax.random.fold_in(key, 6), axis_at), (parts,), jnp.float32, smallest / len(shards), high / len(shards))
        return jnp.repeat(jnp.exp(steps), dims[axis_at] // parts).reshape((-1,) + (1,) * (len(dims) - axis_at - 1))

    gain = one(*shards[0])
    for cut in shards[1:]:
        gain = gain * one(*cut)
    return gain


def noise(rng, extent, scale, reach, split=(), kind=jnp.bfloat16):
    loudness = level_of(rng, extent, split, -0.22, 0.18) if split else 1.0
    values = jax.random.normal(rng, extent, jnp.float32) * scale * loudness
    return jnp.minimum(jnp.maximum(values, -reach), reach).astype(kind)


def setup_inputs(seed: int = 0) -> dict:
    key_of = jax.random.split(jax.random.key(seed), 8)
    return {
        "features": noise(key_of[0], (GROUPS, GROUP_ROWS, DIN), 1.0, 6.0, ((0, 8), (1, 64))),
        "bases": noise(key_of[1], (NBASES, DIN, DOUT), DIN ** -0.5, 0.21875, ((1, 64), (2, 8))),
        "coefficients": noise(key_of[2], (RELS + 1, NBASES), (NBASES * (RELS + 1)) ** -0.5, 0.4375, (), jnp.float32),
        "tile_values": noise(key_of[3], (STRETCHES, GROUPS, SLOTS, DEST, TILE), (4 * TILE * SLOTS) ** -0.5, 0.03125, ((0, 64), (1, 8))),
        "tile_source": touch_ends(jax.random.randint(key_of[4], (STRETCHES, GROUPS, SLOTS), 0, SRC_BLOCKS), jax.random.fold_in(key_of[4], 1), 0, SRC_BLOCKS - 1).astype(jnp.int32),
        "tile_relation": touch_ends(jax.random.randint(key_of[5], (STRETCHES, GROUPS, SLOTS), 0, RELS), jax.random.fold_in(key_of[5], 1), 0, RELS - 1).astype(jnp.int32),
        "tile_count": draw_tile_count(jax.random.fold_in(key_of[7], 71), 0),
    }


def reference(features, bases, coefficients, tile_values, tile_source, tile_relation, tile_count):
    stacked = jnp.dot(coefficients, bases.reshape(NBASES, DIN * DOUT).astype(jnp.float32), precision=lax.Precision.HIGHEST)
    weights = stacked.astype(jnp.bfloat16).reshape((RELS + 1) * DIN, DOUT)
    blocks = features.reshape(GROUPS, SRC_BLOCKS, TILE, DIN)
    slot_ids = jnp.arange(SLOTS, dtype=jnp.int32)
    rel_ids = jnp.arange(RELS, dtype=jnp.int32)

    def one_stretch(stretch_index):
        def one_group(aggregate, group_index):
            live_slots = slot_ids < tile_count[stretch_index, group_index]
            picked = jnp.take(blocks[group_index], tile_source[stretch_index, group_index], axis=0)
            products = jnp.einsum("sab,sbd->sad", tile_values[stretch_index, group_index].astype(jnp.float32), picked.astype(jnp.float32))
            select = ((tile_relation[stretch_index, group_index][:, None] == rel_ids[None, :]) & live_slots[:, None]).astype(jnp.float32)
            return aggregate + jnp.einsum("sr,sad->ard", select, products), None

        aggregate, _ = lax.scan(one_group, jnp.zeros((DEST, RELS, DIN), jnp.float32), jnp.arange(GROUPS, dtype=jnp.int32))
        own_rows = lax.dynamic_slice_in_dim(features, stretch_index * ROWS, ROWS, 1).reshape(DEST, 1, DIN)
        messages = jnp.concatenate([aggregate.astype(jnp.bfloat16), own_rows], axis=1).reshape(DEST, (RELS + 1) * DIN)
        output = jnp.dot(messages, weights, preferred_element_type=jnp.float32)
        return jnp.maximum(output, 0.0).astype(jnp.bfloat16)

    blocks_out = lax.map(one_stretch, jnp.arange(STRETCHES, dtype=jnp.int32))
    return blocks_out.reshape(STRETCHES, GROUPS, ROWS, DOUT).transpose(1, 0, 2, 3).reshape(GROUPS, GROUP_ROWS, DOUT)
```

```python
import functools

import jax
import jax.numpy as jnp
from jax import lax
from jax.experimental import pallas as pl
from jax.experimental.pallas import tpu as pltpu
from jax.sharding import Mesh
from jax.sharding import PartitionSpec as P

BF = jnp.bfloat16
F32 = jnp.float32
NODE = ("y", "x", "zl")
REL = ("zh", "core")
YX = ("y", "x")
VMEM = pl.BlockSpec(memory_space=pltpu.VMEM)
SMEM = pl.BlockSpec(memory_space=pltpu.SMEM)
PARAMS = pltpu.CompilerParams(vmem_limit_bytes=40 * 1024 * 1024)

RELS = 5
DIN = 768
DOUT = 1024
TILE = 128
SRC = 8
ROWS = 16
NODES = 64
PER = 12
SLOT = 8
SELF = 2
CHUNK = SLOT * NODES


def call(body, outs, ins, scratch=()):
    return pl.pallas_call(
        body,
        out_shape=outs,
        in_specs=ins,
        out_specs=jax.tree.map(lambda _: VMEM, outs),
        scratch_shapes=list(scratch),
        compiler_params=PARAMS,
    )


def shape(dims, kind):
    return jax.ShapeDtypeStruct(dims, kind)


def prepare(coef, own, bases, copies, parcel):
    src = lax.broadcasted_iota(jnp.int32, (DIN, DIN), 0)
    out = lax.broadcasted_iota(jnp.int32, (DIN, DIN), 1)
    swap = jnp.where(src == PER * (out & (NODES - 1)) + (out >> 6), 1.0, 0.0).astype(BF)
    turned = jnp.dot(own[...], swap, preferred_element_type=F32).astype(BF)
    for i in range(4):
        copies[i] = turned
    parcel[...] = jnp.zeros_like(parcel)
    for k in range(DIN // TILE):
        parcel[k, :ROWS] = turned[:, k * TILE : (k + 1) * TILE]
    flat = []
    for r in range(RELS + 1):
        total = jnp.zeros((PER, TILE), F32)
        for b in range(bases.shape[0]):
            total = total + coef[r, b] * bases[b].astype(F32)
        flat.append(total)
    rows = jnp.concatenate(flat[:RELS] + [jnp.zeros((4, TILE), F32)], axis=0)
    for k in range(8):
        parcel[k, ROWS : ROWS + SLOT] = rows[k * SLOT : (k + 1) * SLOT].astype(BF)
    for k in range(PER // SELF):
        parcel[k, ROWS + SLOT : ROWS + SLOT + SELF] = flat[RELS][k * SELF : (k + 1) * SELF].astype(BF)


def densify(count, source, relation, values, dense, acc):
    acc[...] = jnp.zeros_like(acc)

    def add(t, _):
        spot = relation[t] * SRC + source[t]
        acc[spot] = acc[spot] + values[t].astype(F32)
        return 0

    lax.fori_loop(0, count[0], add, 0)
    for r in range(RELS):
        for s in range(SRC):
            dense[r, :, s * TILE : (s + 1) * TILE] = acc[r * SRC + s].astype(BF)


def aggregate(core, dense, feats, send, keep, full):
    for r in range(RELS):
        full[:, r * DIN : (r + 1) * DIN] = jnp.dot(dense[r], feats[...], preferred_element_type=F32)
    full[:, RELS * DIN :] = jnp.zeros((TILE, 8 * CHUNK - RELS * DIN), F32)

    def split(mine):
        for z in range(4):
            a = (2 * z + mine) * CHUNK
            b = (2 * z + 1 - mine) * CHUNK
            keep[z] = full[:, a : a + CHUNK]
            send[z] = full[:, b : b + CHUNK].astype(BF)

    @pl.when(core[0] == 0)
    def _():
        split(0)

    @pl.when(core[0] == 1)
    def _():
        split(1)


def pair_sum(keep, got, out):
    out[...] = (keep[...] + got[...].astype(F32)).astype(BF)


def transform(core, got, own, weights, send, keep):
    src = lax.broadcasted_iota(jnp.int32, (CHUNK + TILE, DIN), 0)
    out = lax.broadcasted_iota(jnp.int32, (CHUNK + TILE, DIN), 1)
    swap = jnp.where(out == PER * (src & (NODES - 1)) + (src >> 6), 1.0, 0.0).astype(BF)
    total = got[0].astype(F32)
    for i in range(1, 4):
        total = total + got[i].astype(F32)
    msgs = jnp.concatenate([total.astype(BF), own[...]], axis=1)
    msgs = jnp.dot(msgs, swap, preferred_element_type=F32).astype(BF)
    part = jnp.dot(msgs, weights[...], preferred_element_type=F32)

    def split(mine):
        for z in range(4):
            a = (2 * z + mine) * ROWS
            b = (2 * z + 1 - mine) * ROWS
            keep[z] = part[a : a + ROWS]
            send[z] = part[b : b + ROWS].astype(BF)

    @pl.when(core[0] == 0)
    def _():
        split(0)

    @pl.when(core[0] == 1)
    def _():
        split(1)


def finish(got, out):
    total = got[0].astype(F32)
    for i in range(1, 4):
        total = total + got[i].astype(F32)
    out[...] = jnp.maximum(total, 0.0).astype(BF)


def exchange(x, axis):
    return lax.all_to_all(x, axis, split_axis=0, concat_axis=0, tiled=True)


def spread(x, axis):
    return exchange(jnp.broadcast_to(x, (lax.axis_size(axis), *x.shape)), axis)


def swap_core(x):
    return lax.ppermute(x, "core", [(0, 1), (1, 0)])


def on_device(features, bases, coefficients, tile_values, tile_source, tile_relation, tile_count):
    core = lax.axis_index("core").astype(jnp.int32).reshape(1)
    copies, parcel = call(
        prepare,
        (shape((4, ROWS, DIN), BF), shape((8, 32, TILE), BF)),
        [SMEM, VMEM, VMEM],
    )(coefficients, features[0], bases)
    feats = exchange(copies, "zl").reshape(NODES, DIN)
    feats = spread(feats, YX).reshape(SRC * TILE, DIN)

    dense = call(
        densify,
        shape((RELS, TILE, SRC * TILE), BF),
        [SMEM, SMEM, SMEM, VMEM],
        [pltpu.VMEM((RELS * SRC, TILE, TILE), F32)],
    )(tile_count[0], tile_source[0, 0], tile_relation[0, 0], tile_values[0, 0])
    send, keep = call(
        aggregate,
        (shape((4, TILE, CHUNK), BF), shape((4, TILE, CHUNK), F32)),
        [SMEM, VMEM, VMEM],
        [pltpu.VMEM((TILE, 8 * CHUNK), F32)],
    )(core, dense, feats)
    pair = call(pair_sum, shape((4, TILE, CHUNK), BF), [VMEM, VMEM])(keep, swap_core(send))

    parcel = exchange(parcel, REL)
    own = parcel[:, :ROWS].reshape(TILE, TILE)
    rows = jnp.moveaxis(parcel[:, ROWS : ROWS + PER], 0, 1).reshape(PER, DOUT)
    rows = spread(rows, "zl").reshape(4 * PER, DOUT)
    weights = spread(rows, YX).reshape(NODES * PER, DOUT)

    sums = exchange(pair, "zh")
    send, keep = call(
        transform,
        (shape((4, ROWS, DOUT), BF), shape((4, ROWS, DOUT), F32)),
        [SMEM, VMEM, VMEM, VMEM],
    )(core, sums, own, weights)
    pair = call(pair_sum, shape((4, ROWS, DOUT), BF), [VMEM, VMEM])(keep, swap_core(send))
    return call(finish, shape((ROWS, DOUT), BF), [VMEM])(exchange(pair, "zh"))[None]


def solution(mesh):
    split = Mesh(mesh.devices.reshape(4, 4, 4, 4, 2), NODE + REL)
    return jax.shard_map(
        on_device,
        mesh=split,
        in_specs=(
            P(REL, NODE, None),
            P(None, NODE, REL),
            P(),
            P(NODE, REL, None, None, None),
            P(NODE, REL, None),
            P(NODE, REL, None),
            P(NODE, REL),
        ),
        out_specs=P(REL, NODE, None),
        check_vma=False,
    )
```

```python
import jax
import jax.numpy as jnp
from jax import lax
from jax.experimental import pallas as pl
from jax.experimental.pallas import tpu as pltpu
from jax.sharding import Mesh
from jax.sharding import PartitionSpec as P

BF = jnp.bfloat16
F32 = jnp.float32
NODE = ("y", "x", "zl")
REL = ("zh", "core")
YX = ("y", "x")
VMEM = pl.BlockSpec(memory_space=pltpu.VMEM)
SMEM = pl.BlockSpec(memory_space=pltpu.SMEM)
PARAMS = pltpu.CompilerParams(vmem_limit_bytes=40 * 1024 * 1024)

RELS = 5
DIN = 768
DOUT = 1024
TILE = 128
SRC = 8
ROWS = 16
NODES = 64
PER = 12
SLOT = 8
SELF = 2
CHUNK = SLOT * NODES
HALF = TILE // 2


def call(body, outs, ins, scratch=()):
    return pl.pallas_call(
        body,
        out_shape=outs,
        in_specs=ins,
        out_specs=jax.tree.map(lambda _: VMEM, outs),
        scratch_shapes=list(scratch),
        compiler_params=PARAMS,
    )


def shape(kind, *dims):
    return jax.ShapeDtypeStruct(dims, kind)


def turn(own, turned, copies):
    src = lax.broadcasted_iota(jnp.int32, (DIN, DIN), 0)
    out = lax.broadcasted_iota(jnp.int32, (DIN, DIN), 1)
    swap = jnp.where(src == PER * (out & (NODES - 1)) + (out >> 6), 1.0, 0.0).astype(BF)
    value = jnp.dot(own[...], swap, preferred_element_type=F32).astype(BF)
    turned[...] = value
    for i in range(4):
        copies[i] = value


def weigh(place, coef, turned, bases, send, keep, parcel):
    parcel[...] = jnp.zeros_like(parcel)
    for k in range(DIN // TILE):
        parcel[k, :ROWS] = turned[:, k * TILE : (k + 1) * TILE]
    flat = []
    for r in range(RELS + 1):
        total = jnp.zeros((PER, TILE), F32)
        for b in range(bases.shape[0]):
            total = total + coef[r, b] * bases[b].astype(F32)
        flat.append(total)
    rows = jnp.concatenate(flat[:RELS] + [jnp.zeros((4, TILE), F32)], axis=0)
    for k in range(8):
        parcel[k, ROWS : ROWS + SLOT] = rows[k * SLOT : (k + 1) * SLOT].astype(BF)
    for k in range(PER // SELF):
        parcel[k, ROWS + SLOT : ROWS + SLOT + SELF] = flat[RELS][k * SELF : (k + 1) * SELF].astype(BF)
    zh, core = place[1], place[2]
    for d in range(4):
        z = 2 * lax.rem(zh + d, 4)
        keep[d] = parcel[z + core]
        send[d] = parcel[z + 1 - core]


def join_cores(place, keep, got, *outs):
    core = place[2]
    for d in range(4):
        outs[d][core] = keep[d]
        outs[d][1 - core] = got[d]


def join_groups(place, *refs):
    ins, (own, rows) = refs[:4], refs[4:]
    for d in range(4):
        z = lax.rem(place[1] + 4 - d, 4)
        for c in range(2):
            g = 2 * z + c
            own[g] = ins[d][c, :ROWS]
            rows[:, pl.ds(pl.multiple_of(g * TILE, TILE), TILE)] = ins[d][c, ROWS:]


def stack(a, b, c, d, out):
    out[...] = jnp.concatenate([x[:PER].astype(F32) for x in (a, b, c, d)], axis=0).astype(BF)


def densify(count, source, relation, values, dense, acc):
    acc[...] = jnp.zeros_like(acc)

    def add(t, _):
        spot = relation[t] * SRC + source[t]
        acc[spot] = acc[spot] + values[t].astype(F32)
        return 0

    lax.fori_loop(0, count[0], add, 0)
    for r in range(RELS):
        for s in range(SRC):
            dense[r, :, s * TILE : (s + 1) * TILE] = acc[r * SRC + s].astype(BF)


def aggregate(place, dense, feats, send, keep, full):
    for r in range(RELS):
        full[:, r * DIN : (r + 1) * DIN] = jnp.dot(dense[r], feats[...], preferred_element_type=F32)
    full[:, RELS * DIN :] = jnp.zeros((TILE, 8 * CHUNK - RELS * DIN), F32)
    zh, core = place[1], place[2]
    for e in range(4):
        z = 2 * (zh ^ e)
        keep[e] = full[:, pl.ds(pl.multiple_of((z + core) * CHUNK, CHUNK), CHUNK)]
        send[e] = full[:, pl.ds(pl.multiple_of((z + 1 - core) * CHUNK, CHUNK), CHUNK)].astype(BF)


def first_half(keep, got, send_a, send_b, keep_a, keep_b):
    def total(e, rows):
        return keep[e, rows] + got[e, rows].astype(F32)

    a, b = slice(0, HALF), slice(HALF, TILE)
    send_a[0] = total(1, a).astype(BF)
    send_a[1] = total(2, a).astype(BF)
    send_b[0] = total(3, b).astype(BF)
    send_b[1] = total(2, b).astype(BF)
    keep_a[0] = total(0, a)
    keep_a[1] = total(3, a)
    keep_b[0] = total(0, b)
    keep_b[1] = total(1, b)


def second_half(keep_a, keep_b, got_a, got_b, send_a, send_b, hold):
    hold[:HALF] = keep_a[0] + got_a[0].astype(F32)
    hold[HALF:] = keep_b[0] + got_b[0].astype(F32)
    send_a[...] = (keep_a[1] + got_a[1].astype(F32)).astype(BF)
    send_b[...] = (keep_b[1] + got_b[1].astype(F32)).astype(BF)


def transform(place, hold, got_a, got_b, own, weights, send, keep, part):
    zl, core = place[0], place[2]
    src = lax.broadcasted_iota(jnp.int32, (CHUNK + TILE, DIN), 0)
    out = lax.broadcasted_iota(jnp.int32, (CHUNK + TILE, DIN), 1)
    node = src & (NODES - 1)
    spot = 4 * PER * (node >> 2) + PER * ((zl - node) & 3) + (src >> 6)
    swap = jnp.where(out == spot, 1.0, 0.0).astype(BF)
    top = (hold[:HALF] + got_a[...].astype(F32)).astype(BF)
    low = (hold[HALF:] + got_b[...].astype(F32)).astype(BF)
    msgs = jnp.concatenate([jnp.concatenate([top, low], axis=0), own[...]], axis=1)
    msgs = jnp.dot(msgs, swap, preferred_element_type=F32).astype(BF)
    part[...] = jnp.dot(msgs, weights[...], preferred_element_type=F32)
    for z in range(4):
        keep[z] = part[pl.ds(pl.multiple_of((2 * z + core) * ROWS, ROWS), ROWS)]
        send[z] = part[pl.ds(pl.multiple_of((2 * z + 1 - core) * ROWS, ROWS), ROWS)].astype(BF)


def pair_sum(keep, got, out):
    out[...] = (keep[...] + got[...].astype(F32)).astype(BF)


def finish(got, out):
    total = got[0].astype(F32)
    for i in range(1, 4):
        total = total + got[i].astype(F32)
    out[...] = jnp.maximum(total, 0.0).astype(BF)


def exchange(x, axis):
    return lax.all_to_all(x, axis, split_axis=0, concat_axis=0, tiled=True)


def spread(x, axis):
    return exchange(jnp.broadcast_to(x, (lax.axis_size(axis), *x.shape)), axis)


def shift(x, axis, step):
    return lax.ppermute(x, axis, [(i, (i + step) % 4) for i in range(4)])


def partner(x, axis, mask):
    return lax.ppermute(x, axis, [(i, i ^ mask) for i in range(lax.axis_size(axis))])


def on_device(features, bases, coefficients, tile_values, tile_source, tile_relation, tile_count):
    place = jnp.stack([lax.axis_index(a) for a in ("zl", "zh", "core")]).astype(jnp.int32)
    turned, copies = call(
        turn, (shape(BF, ROWS, DIN), shape(BF, 4, ROWS, DIN)), [VMEM]
    )(features[0])
    feats = exchange(copies, "zl").reshape(NODES, DIN)

    send, keep = call(
        weigh,
        (shape(BF, 4, 32, TILE), shape(BF, 4, 32, TILE)),
        [SMEM, SMEM, VMEM, VMEM],
        [pltpu.VMEM((8, 32, TILE), BF)],
    )(place, coefficients, turned, bases)
    block = shape(BF, 2, 32, TILE)
    parts = call(join_cores, (block,) * 4, [SMEM, VMEM, VMEM])(place, keep, partner(send, "core", 1))
    parts = [parts[0]] + [shift(parts[d], "zh", d) for d in (1, 2, 3)]

    feats = spread(feats, YX).reshape(SRC * TILE, DIN)

    own, rows = call(
        join_groups,
        (shape(BF, 8, ROWS, TILE), shape(BF, ROWS, DOUT)),
        [SMEM] + [VMEM] * 4,
    )(place, *parts)
    own = own.reshape(TILE, TILE)
    rows = [rows] + [shift(rows, "zl", d) for d in (1, 2, 3)]
    rows = call(stack, shape(BF, 4 * PER, DOUT), [VMEM] * 4)(*rows)
    weights = spread(rows, YX).reshape(NODES * PER, DOUT)

    dense = call(
        densify,
        shape(BF, RELS, TILE, SRC * TILE),
        [SMEM, SMEM, SMEM, VMEM],
        [pltpu.VMEM((RELS * SRC, TILE, TILE), F32)],
    )(tile_count[0], tile_source[0, 0], tile_relation[0, 0], tile_values[0, 0])
    send, keep = call(
        aggregate,
        (shape(BF, 4, TILE, CHUNK), shape(F32, 4, TILE, CHUNK)),
        [SMEM, VMEM, VMEM],
        [pltpu.VMEM((TILE, 8 * CHUNK), F32)],
    )(place, dense, feats)
    two = shape(BF, 2, HALF, CHUNK)
    wide = shape(F32, 2, HALF, CHUNK)
    send_a, send_b, keep_a, keep_b = call(first_half, (two, two, wide, wide), [VMEM] * 2)(
        keep, partner(send, "core", 1)
    )
    one = shape(BF, HALF, CHUNK)
    send_a, send_b, hold = call(second_half, (one, one, shape(F32, TILE, CHUNK)), [VMEM] * 4)(
        keep_a, keep_b, partner(send_a, "zh", 1), partner(send_b, "zh", 3)
    )
    send, keep = call(
        transform,
        (shape(BF, 4, ROWS, DOUT), shape(F32, 4, ROWS, DOUT)),
        [SMEM] + [VMEM] * 5,
        [pltpu.VMEM((TILE, DOUT), F32)],
    )(place, hold, partner(send_a, "zh", 3), partner(send_b, "zh", 1), own, weights)
    pair = call(pair_sum, shape(BF, 4, ROWS, DOUT), [VMEM] * 2)(keep, partner(send, "core", 1))
    return call(finish, shape(BF, ROWS, DOUT), [VMEM])(exchange(pair, "zh"))[None]


def solution(mesh):
    split = Mesh(mesh.devices.reshape(4, 4, 4, 4, 2), NODE + REL)
    return jax.shard_map(
        on_device,
        mesh=split,
        in_specs=(
            P(REL, NODE, None),
            P(None, NODE, REL),
            P(),
            P(NODE, REL, None, None, None),
            P(NODE, REL, None),
            P(NODE, REL, None),
            P(NODE, REL),
        ),
        out_specs=P(REL, NODE, None),
        check_vma=False,
    )
```

```python
import jax
import jax.numpy as jnp
from jax import lax
from jax.experimental import pallas as pl
from jax.experimental.pallas import tpu as pltpu
from jax.sharding import Mesh
from jax.sharding import PartitionSpec as P

BF = jnp.bfloat16
F32 = jnp.float32
NODE = ("y", "x", "zl")
REL = ("zh", "core")
YX = ("y", "x")
VMEM = pl.BlockSpec(memory_space=pltpu.VMEM)
ANY = pl.BlockSpec(memory_space=pl.ANY)
HBM = pl.BlockSpec(memory_space=pltpu.HBM)
SMEM = pl.BlockSpec(memory_space=pltpu.SMEM)
PARAMS = pltpu.CompilerParams(vmem_limit_bytes=16 * 1024 * 1024)

RELS = 5
DIN = 768
DOUT = 1024
TILE = 128
SRC = 8
ROWS = 16
NODES = 64
PER = 12
SLOT = 8
SELF = 2
CHUNK = SLOT * NODES
HALF = TILE // 2


def call(body, outs, ins, scratch=(), where=VMEM):
    return pl.pallas_call(
        body,
        out_shape=outs,
        in_specs=ins,
        out_specs=jax.tree.map(lambda _: where, outs),
        scratch_shapes=list(scratch),
        compiler_params=PARAMS,
    )


def shape(kind, *dims):
    return jax.ShapeDtypeStruct(dims, kind)


def start(own, coef, bases, padded, copies, rows):
    src = lax.broadcasted_iota(jnp.int32, (DIN, DIN), 0)
    out = lax.broadcasted_iota(jnp.int32, (DIN, DIN), 1)
    swap = jnp.where(src == PER * (out & (NODES - 1)) + (out >> 6), 1.0, 0.0).astype(BF)
    value = jnp.dot(own[...], swap, preferred_element_type=F32).astype(BF)
    padded[:, :DIN] = value
    padded[:, DIN:] = jnp.zeros((ROWS, 8 * TILE - DIN), BF)
    rows[...] = jnp.zeros_like(rows)
    for d in range(PER):
        part = jnp.dot(
            coef[...], bases[d].astype(F32), precision=lax.Precision.HIGHEST, preferred_element_type=F32
        )
        for r in range(RELS):
            j = r * PER + d
            rows[j // SLOT, j % SLOT : j % SLOT + 1] = part[r : r + 1]
        rows[d // SELF, SLOT + d % SELF : SLOT + d % SELF + 1] = part[RELS :]
    for i in range(4):
        copies[i, :, :DIN] = value
        for k in range(8):
            copies[i, :, DIN + k * TILE : DIN + (k + 1) * TILE] = rows[k].astype(BF)


def repeat(block, copies, sems):
    moves = [pltpu.make_async_copy(block, copies.at[i], sems.at[i]) for i in range(copies.shape[0])]
    for move in moves:
        move.start()
    for move in moves:
        move.wait()


def fan(after, gathered, copies, block, sems):
    block[...] = gathered[:, :, :DIN].reshape(NODES, DIN)
    repeat(block, copies, sems)


def fan_rows(after, rows, copies, sems):
    repeat(rows, copies, sems)


def sort(place, padded, gathered, send, keep):
    zh, core = place[0], place[1]

    def fill(ref, d, k):
        ref[d, :ROWS] = padded[:, pl.ds(pl.multiple_of(k * TILE, TILE), TILE)]
        spot = pl.ds(pl.multiple_of(DIN + k * TILE, TILE), TILE)
        rows = [gathered[z, :, spot].astype(F32)[:PER] for z in range(4)]
        ref[d, ROWS:] = jnp.concatenate(rows, axis=0).astype(BF)

    for d in range(4):
        z = 2 * lax.rem(zh + d, 4)
        fill(keep, d, z + core)
        fill(send, d, z + 1 - core)


def join_cores(place, keep, got, *outs):
    core = place[1]
    for d in range(4):
        outs[d][core] = keep[d]
        outs[d][1 - core] = got[d]


def join_groups(place, *refs):
    ins, (own, rows) = refs[:4], refs[4:]
    for d in range(4):
        z = lax.rem(place[0] + 4 - d, 4)
        for c in range(2):
            g = 2 * z + c
            own[g] = ins[d][c, :ROWS]
            rows[:, pl.ds(pl.multiple_of(g * TILE, TILE), TILE)] = ins[d][c, ROWS:]


def densify(count, source, relation, values, dense, acc):
    acc[...] = jnp.zeros_like(acc)

    def add(t, _):
        spot = relation[t] * SRC + source[t]
        acc[spot] = acc[spot] + values[t].astype(F32)
        return 0

    lax.fori_loop(0, count[0], add, 0)
    for r in range(RELS):
        for s in range(SRC):
            dense[r, :, s * TILE : (s + 1) * TILE] = acc[r * SRC + s].astype(BF)


def aggregate(place, dense, feats, after, send, keep, full):
    for r in range(RELS):
        full[:, r * DIN : (r + 1) * DIN] = jnp.dot(dense[r], feats[...], preferred_element_type=F32)
    full[:, RELS * DIN :] = jnp.zeros((TILE, 8 * CHUNK - RELS * DIN), F32)
    zh, core = place[0], place[1]
    for e in range(4):
        z = 2 * (zh ^ e)
        keep[e] = full[:, pl.ds(pl.multiple_of((z + core) * CHUNK, CHUNK), CHUNK)]
        send[e] = full[:, pl.ds(pl.multiple_of((z + 1 - core) * CHUNK, CHUNK), CHUNK)].astype(BF)


def first_half(keep, got, send_a, send_b, keep_a, keep_b):
    def total(e, rows):
        return keep[e, rows] + got[e, rows].astype(F32)

    a, b = slice(0, HALF), slice(HALF, TILE)
    send_a[0] = total(1, a).astype(BF)
    send_a[1] = total(2, a).astype(BF)
    send_b[0] = total(3, b).astype(BF)
    send_b[1] = total(2, b).astype(BF)
    keep_a[0] = total(0, a)
    keep_a[1] = total(3, a)
    keep_b[0] = total(0, b)
    keep_b[1] = total(1, b)


def second_half(keep_a, keep_b, got_a, got_b, send_a, send_b, hold):
    hold[:HALF] = keep_a[0] + got_a[0].astype(F32)
    hold[HALF:] = keep_b[0] + got_b[0].astype(F32)
    send_a[...] = (keep_a[1] + got_a[1].astype(F32)).astype(BF)
    send_b[...] = (keep_b[1] + got_b[1].astype(F32)).astype(BF)


def transform(place, hold, got_a, got_b, own, weights, send, keep, part):
    core = place[1]
    src = lax.broadcasted_iota(jnp.int32, (CHUNK + TILE, DIN), 0)
    out = lax.broadcasted_iota(jnp.int32, (CHUNK + TILE, DIN), 1)
    swap = jnp.where(out == PER * (src & (NODES - 1)) + (src >> 6), 1.0, 0.0).astype(BF)
    top = (hold[:HALF] + got_a[...].astype(F32)).astype(BF)
    low = (hold[HALF:] + got_b[...].astype(F32)).astype(BF)
    msgs = jnp.concatenate([jnp.concatenate([top, low], axis=0), own[...]], axis=1)
    msgs = jnp.dot(msgs, swap, preferred_element_type=F32).astype(BF)
    part[...] = jnp.dot(msgs, weights[...], preferred_element_type=F32)
    for z in range(4):
        keep[z] = part[pl.ds(pl.multiple_of((2 * z + core) * ROWS, ROWS), ROWS)]
        send[z] = part[pl.ds(pl.multiple_of((2 * z + 1 - core) * ROWS, ROWS), ROWS)].astype(BF)


def pair_sum(keep, got, out):
    out[...] = (keep[...] + got[...].astype(F32)).astype(BF)


def finish(got, out):
    total = got[0].astype(F32)
    for i in range(1, 4):
        total = total + got[i].astype(F32)
    out[...] = jnp.maximum(total, 0.0).astype(BF)


def exchange(x, axis):
    return lax.all_to_all(x, axis, split_axis=0, concat_axis=0, tiled=True)


def shift(x, axis, step):
    return lax.ppermute(x, axis, [(i, (i + step) % 4) for i in range(4)])


def partner(x, axis, mask):
    return lax.ppermute(x, axis, [(i, i ^ mask) for i in range(lax.axis_size(axis))])


def on_device(features, bases, coefficients, tile_values, tile_source, tile_relation, tile_count):
    place = jnp.stack([lax.axis_index(a) for a in REL]).astype(jnp.int32)
    padded, copies = call(
        start,
        (shape(BF, ROWS, 8 * TILE), shape(BF, 4, ROWS, DIN + 8 * TILE)),
        [VMEM] * 3,
        [pltpu.VMEM((8, ROWS, TILE), F32)],
    )(features[0], coefficients, jnp.swapaxes(bases, 0, 1))
    gathered = exchange(copies, "zl")
    dense = call(
        densify,
        shape(BF, RELS, TILE, SRC * TILE),
        [SMEM, SMEM, SMEM, VMEM],
        [pltpu.VMEM((RELS * SRC, TILE, TILE), F32)],
    )(tile_count[0], tile_source[0, 0], tile_relation[0, 0], tile_values[0, 0])
    feats = call(
        fan,
        shape(BF, 16, NODES, DIN),
        [ANY, VMEM],
        [pltpu.VMEM((NODES, DIN), BF), pltpu.SemaphoreType.DMA((16,))],
        HBM,
    )(dense, gathered)
    feats = exchange(feats, YX).reshape(SRC * TILE, DIN)

    parcel = shape(BF, 4, ROWS + 4 * PER, TILE)
    send, keep = call(sort, (parcel, parcel), [SMEM, VMEM, VMEM])(place, padded, gathered)
    block = shape(BF, 2, ROWS + 4 * PER, TILE)
    parts = call(join_cores, (block,) * 4, [SMEM, VMEM, VMEM])(place, keep, partner(send, "core", 1))
    parts = [parts[0]] + [shift(parts[d], "zh", d) for d in (1, 2, 3)]
    own, rows = call(
        join_groups,
        (shape(BF, 8, ROWS, TILE), shape(BF, 4 * PER, DOUT)),
        [SMEM] + [VMEM] * 4,
    )(place, *parts)
    own = own.reshape(TILE, TILE)

    send, keep = call(
        aggregate,
        (shape(BF, 4, TILE, CHUNK), shape(F32, 4, TILE, CHUNK)),
        [SMEM, VMEM, VMEM, ANY],
        [pltpu.VMEM((TILE, 8 * CHUNK), F32)],
    )(place, dense, feats, rows)
    weights = call(
        fan_rows,
        shape(BF, 16, 4 * PER, DOUT),
        [ANY, VMEM],
        [pltpu.SemaphoreType.DMA((16,))],
        HBM,
    )(send, rows)
    weights = exchange(weights, YX).reshape(NODES * PER, DOUT)
    two = shape(BF, 2, HALF, CHUNK)
    wide = shape(F32, 2, HALF, CHUNK)
    send_a, send_b, keep_a, keep_b = call(first_half, (two, two, wide, wide), [VMEM] * 2)(
        keep, partner(send, "core", 1)
    )
    one = shape(BF, HALF, CHUNK)
    send_a, send_b, hold = call(second_half, (one, one, shape(F32, TILE, CHUNK)), [VMEM] * 4)(
        keep_a, keep_b, partner(send_a, "zh", 1), partner(send_b, "zh", 3)
    )
    send, keep = call(
        transform,
        (shape(BF, 4, ROWS, DOUT), shape(F32, 4, ROWS, DOUT)),
        [SMEM] + [VMEM] * 5,
        [pltpu.VMEM((TILE, DOUT), F32)],
    )(place, hold, partner(send_a, "zh", 3), partner(send_b, "zh", 1), own, weights)
    pair = call(pair_sum, shape(BF, 4, ROWS, DOUT), [VMEM] * 2)(keep, partner(send, "core", 1))
    return call(finish, shape(BF, ROWS, DOUT), [VMEM])(exchange(pair, "zh"))[None]


def solution(mesh):
    split = Mesh(mesh.devices.reshape(4, 4, 4, 4, 2), NODE + REL)
    return jax.shard_map(
        on_device,
        mesh=split,
        in_specs=(
            P(REL, NODE, None),
            P(None, NODE, REL),
            P(),
            P(NODE, REL, None, None, None),
            P(NODE, REL, None),
            P(NODE, REL, None),
            P(NODE, REL),
        ),
        out_specs=P(REL, NODE, None),
        check_vma=False,
    )
```

```python
import jax
import jax.numpy as jnp
from jax import lax
from jax.experimental import pallas as pl
from jax.experimental.pallas import tpu as pltpu
from jax.sharding import Mesh
from jax.sharding import PartitionSpec as P

BF = jnp.bfloat16
F32 = jnp.float32
NODE = ("y", "x", "zl")
REL = ("zh", "core")
YX = ("y", "x")
VMEM = pl.BlockSpec(memory_space=pltpu.VMEM)
ANY = pl.BlockSpec(memory_space=pl.ANY)
SMEM = pl.BlockSpec(memory_space=pltpu.SMEM)
PARAMS = pltpu.CompilerParams(vmem_limit_bytes=16 * 1024 * 1024)

RELS = 5
DIN = 768
DOUT = 1024
TILE = 128
SRC = 8
ROWS = 16
NODES = 64
PER = 12
SLOT = 8
SELF = 2
CHUNK = SLOT * NODES
WEIGHT = 10**11


def call(body, outs, ins, scratch=(), cost=None):
    return pl.pallas_call(
        body,
        cost_estimate=cost,
        out_shape=outs,
        in_specs=ins,
        out_specs=jax.tree.map(lambda _: VMEM, outs),
        scratch_shapes=list(scratch),
        compiler_params=PARAMS,
    )


def shape(kind, *dims):
    return jax.ShapeDtypeStruct(dims, kind)


def start(own, turned, copies):
    src = lax.broadcasted_iota(jnp.int32, (DIN, DIN), 0)
    out = lax.broadcasted_iota(jnp.int32, (DIN, DIN), 1)
    swap = jnp.where(src == PER * (out & (NODES - 1)) + (out >> 6), 1.0, 0.0).astype(BF)
    value = jnp.dot(own[...], swap, preferred_element_type=F32).astype(BF)
    turned[...] = value
    for i in range(4):
        copies[i] = value


def weigh(place, coef, turned, bases, send, keep, rows, parcel):
    rows[...] = jnp.zeros_like(rows)
    for d in range(PER):
        part = jnp.dot(
            coef[...], bases[d].astype(F32), precision=lax.Precision.HIGHEST, preferred_element_type=F32
        )
        for r in range(RELS):
            j = r * PER + d
            rows[j // SLOT, j % SLOT : j % SLOT + 1] = part[r : r + 1]
        rows[d // SELF, SLOT + d % SELF : SLOT + d % SELF + 1] = part[RELS:]
    for k in range(8):
        if k < DIN // TILE:
            parcel[k, :ROWS] = turned[:, k * TILE : (k + 1) * TILE]
        else:
            parcel[k, :ROWS] = jnp.zeros((ROWS, TILE), BF)
        parcel[k, ROWS:] = rows[k].astype(BF)
    core = place[0]
    for z in range(4):
        keep[z] = parcel[2 * z + core]
        send[z] = parcel[2 * z + 1 - core]


def join_cores(place, after, keep, got, out):
    core = place[0]
    mine = pl.ds(pl.multiple_of(core * TILE, TILE), TILE)
    other = pl.ds(pl.multiple_of((1 - core) * TILE, TILE), TILE)
    for z in range(4):
        for i in range(4):
            out[4 * z + i, :, mine] = keep[z]
            out[4 * z + i, :, other] = got[z]


def join_groups(place, got, own, rows):
    zl = place[1]
    for z in range(4):
        for c in range(2):
            own[2 * z + c] = got[4 * z + zl, :ROWS, c * TILE : (c + 1) * TILE]
        part = [got[4 * z + i, ROWS:].astype(F32)[:PER] for i in range(4)]
        rows[:, 2 * z * TILE : 2 * (z + 1) * TILE] = jnp.concatenate(part, axis=0).astype(BF)


def densify(count, source, relation, values, dense, acc):
    acc[...] = jnp.zeros_like(acc)

    def add(t, _):
        spot = relation[t] * SRC + source[t]
        acc[spot] = acc[spot] + values[t].astype(F32)
        return 0

    lax.fori_loop(0, count[0], add, 0)
    for r in range(RELS):
        for s in range(SRC):
            dense[r, :, s * TILE : (s + 1) * TILE] = acc[r * SRC + s].astype(BF)


def aggregate(place, dense, feats, send, keep, full):
    for r in range(RELS):
        full[:, r * DIN : (r + 1) * DIN] = jnp.dot(dense[r], feats[...], preferred_element_type=F32)
    full[:, RELS * DIN :] = jnp.zeros((TILE, 8 * CHUNK - RELS * DIN), F32)
    core = place[0]
    for z in range(4):
        keep[z] = full[:, pl.ds(pl.multiple_of((2 * z + core) * CHUNK, CHUNK), CHUNK)]
        send[z] = full[:, pl.ds(pl.multiple_of((2 * z + 1 - core) * CHUNK, CHUNK), CHUNK)].astype(BF)


def arrange(sums, own, msgs):
    src = lax.broadcasted_iota(jnp.int32, (CHUNK + TILE, DIN), 0)
    out = lax.broadcasted_iota(jnp.int32, (CHUNK + TILE, DIN), 1)
    swap = jnp.where(out == PER * (src & (NODES - 1)) + (src >> 6), 1.0, 0.0).astype(BF)
    value = jnp.concatenate([sums[...], own[...]], axis=1)
    msgs[...] = jnp.dot(value, swap, preferred_element_type=F32).astype(BF)


def transform(place, msgs, weights, send, keep, part):
    core = place[0]
    part[...] = jnp.dot(msgs[...], weights[...], preferred_element_type=F32)
    for z in range(4):
        keep[z] = part[pl.ds(pl.multiple_of((2 * z + core) * ROWS, ROWS), ROWS)]
        send[z] = part[pl.ds(pl.multiple_of((2 * z + 1 - core) * ROWS, ROWS), ROWS)].astype(BF)


def pair_sum(keep, got, out):
    out[...] = (keep[...] + got[...].astype(F32)).astype(BF)


def finish(got, out):
    total = got[0].astype(F32)
    for i in range(1, 4):
        total = total + got[i].astype(F32)
    out[...] = jnp.maximum(total, 0.0).astype(BF)


def exchange(x, axis):
    return lax.all_to_all(x, axis, split_axis=0, concat_axis=0, tiled=True)


def spread(x, axis):
    return exchange(jnp.broadcast_to(x, (lax.axis_size(axis), *x.shape)), axis)


def partner(x):
    return lax.ppermute(x, "core", [(0, 1), (1, 0)])


def on_device(features, bases, coefficients, tile_values, tile_source, tile_relation, tile_count):
    place = jnp.stack([lax.axis_index(a) for a in ("core", "zl")]).astype(jnp.int32)
    turned, copies = call(
        start, (shape(BF, ROWS, DIN), shape(BF, 4, ROWS, DIN)), [VMEM]
    )(features[0])
    feats = exchange(copies, "zl").reshape(NODES, DIN)
    feats = spread(feats, YX).reshape(SRC * TILE, DIN)

    dense = call(
        densify,
        shape(BF, RELS, TILE, SRC * TILE),
        [SMEM, SMEM, SMEM, VMEM],
        [pltpu.VMEM((RELS * SRC, TILE, TILE), F32)],
    )(tile_count[0], tile_source[0, 0], tile_relation[0, 0], tile_values[0, 0])
    part = shape(F32, 4, TILE, CHUNK)
    send, keep = call(
        aggregate,
        (shape(BF, 4, TILE, CHUNK), part),
        [SMEM, VMEM, VMEM],
        [pltpu.VMEM((TILE, 8 * CHUNK), F32)],
    )(place, dense, feats)
    pair = call(pair_sum, shape(BF, 4, TILE, CHUNK), [VMEM] * 2)(keep, partner(send))
    sums = lax.psum_scatter(pair.reshape(4 * TILE, CHUNK), "zh", scatter_dimension=0, tiled=True)

    parcel = shape(BF, 4, 2 * ROWS, TILE)
    send, keep = call(
        weigh,
        (parcel, parcel),
        [SMEM] + [VMEM] * 3,
        [pltpu.VMEM((8, ROWS, TILE), F32), pltpu.VMEM((8, 2 * ROWS, TILE), BF)],
    )(place, coefficients, turned, jnp.swapaxes(bases, 0, 1))
    joined = call(join_cores, shape(BF, 16, 2 * ROWS, 2 * TILE), [SMEM, ANY, VMEM, VMEM])(
        place, pair, keep, partner(send)
    )
    own, rows = call(
        join_groups,
        (shape(BF, 8, ROWS, TILE), shape(BF, 4 * PER, DOUT)),
        [SMEM, VMEM],
    )(place, exchange(joined, ("zh", "zl")))
    weights = spread(rows, YX).reshape(NODES * PER, DOUT)
    msgs = call(
        arrange,
        shape(BF, TILE, DIN),
        [VMEM] * 2,
        cost=pl.CostEstimate(flops=WEIGHT, bytes_accessed=1 << 20, transcendentals=0),
    )(sums, own.reshape(TILE, TILE))

    send, keep = call(
        transform,
        (shape(BF, 4, ROWS, DOUT), shape(F32, 4, ROWS, DOUT)),
        [SMEM] + [VMEM] * 2,
        [pltpu.VMEM((TILE, DOUT), F32)],
    )(place, msgs, weights)
    pair = call(pair_sum, shape(BF, 4, ROWS, DOUT), [VMEM] * 2)(keep, partner(send))
    return call(finish, shape(BF, ROWS, DOUT), [VMEM])(exchange(pair, "zh"))[None]


def solution(mesh):
    split = Mesh(mesh.devices.reshape(4, 4, 4, 4, 2), NODE + REL)
    return jax.shard_map(
        on_device,
        mesh=split,
        in_specs=(
            P(REL, NODE, None),
            P(None, NODE, REL),
            P(),
            P(NODE, REL, None, None, None),
            P(NODE, REL, None),
            P(NODE, REL, None),
            P(NODE, REL),
        ),
        out_specs=P(REL, NODE, None),
        check_vma=False,
    )
```

```python
import jax
import jax.numpy as jnp
from jax import lax
from jax.experimental import pallas as pl
from jax.experimental.pallas import tpu as pltpu
from jax.sharding import Mesh
from jax.sharding import PartitionSpec as P

BF = jnp.bfloat16
F32 = jnp.float32
NODE = ("y", "x", "zl")
REL = ("zh", "core")
YX = ("y", "x")
VMEM = pl.BlockSpec(memory_space=pltpu.VMEM)
ANY = pl.BlockSpec(memory_space=pl.ANY)
SMEM = pl.BlockSpec(memory_space=pltpu.SMEM)
PARAMS = pltpu.CompilerParams(vmem_limit_bytes=16 * 1024 * 1024)

RELS = 5
DIN = 768
DOUT = 1024
TILE = 128
SRC = 8
ROWS = 16
NODES = 64
PER = 12
SLOT = 8
SELF = 2
CHUNK = SLOT * NODES
WEIGHT = 10**11


def call(body, outs, ins, scratch=(), cost=None):
    return pl.pallas_call(
        body,
        cost_estimate=cost,
        out_shape=outs,
        in_specs=ins,
        out_specs=jax.tree.map(lambda _: VMEM, outs),
        scratch_shapes=list(scratch),
        compiler_params=PARAMS,
    )


def shape(kind, *dims):
    return jax.ShapeDtypeStruct(dims, kind)


def start(own, coef, bases, padded, copies, rows):
    src = lax.broadcasted_iota(jnp.int32, (DIN, DIN), 0)
    out = lax.broadcasted_iota(jnp.int32, (DIN, DIN), 1)
    swap = jnp.where(src == PER * (out & (NODES - 1)) + (out >> 6), 1.0, 0.0).astype(BF)
    value = jnp.dot(own[...], swap, preferred_element_type=F32).astype(BF)
    padded[:, :DIN] = value
    padded[:, DIN:] = jnp.zeros((ROWS, 8 * TILE - DIN), BF)
    rows[...] = jnp.zeros_like(rows)
    for d in range(PER):
        part = jnp.dot(
            coef[...], bases[d].astype(F32), precision=lax.Precision.HIGHEST, preferred_element_type=F32
        )
        for r in range(RELS):
            j = r * PER + d
            rows[j // SLOT, j % SLOT : j % SLOT + 1] = part[r : r + 1]
        rows[d // SELF, SLOT + d % SELF : SLOT + d % SELF + 1] = part[RELS :]
    for i in range(4):
        copies[i, :, :DIN] = value
        for k in range(8):
            copies[i, :, DIN + k * TILE : DIN + (k + 1) * TILE] = rows[k].astype(BF)


def sort(place, padded, gathered, send, keep):
    core = place[1]

    def fill(ref, z, k):
        ref[z, :ROWS] = padded[:, pl.ds(pl.multiple_of(k * TILE, TILE), TILE)]
        spot = pl.ds(pl.multiple_of(DIN + k * TILE, TILE), TILE)
        rows = [gathered[i, :, spot].astype(F32)[:PER] for i in range(4)]
        ref[z, ROWS:] = jnp.concatenate(rows, axis=0).astype(BF)

    for z in range(4):
        fill(keep, z, 2 * z + core)
        fill(send, z, 2 * z + 1 - core)


def join_cores(place, keep, got, send, mine, relay):
    zh, core = place[0], place[1]
    for e, ref in ((1, send.at[0]), (2, send.at[1]), (0, mine), (3, relay)):
        z = zh ^ e
        ref[core] = keep[z]
        ref[1 - core] = got[z]


def pass_on(relay, got, send):
    send[0] = relay[...]
    send[1] = got[1]


def join_groups(place, mine, first, second, own, rows):
    for e, ref in ((0, mine), (1, first.at[0]), (3, second.at[0]), (2, second.at[1])):
        z = place[0] ^ e
        for c in range(2):
            g = 2 * z + c
            own[g] = ref[c, :ROWS]
            rows[:, pl.ds(pl.multiple_of(g * TILE, TILE), TILE)] = ref[c, ROWS:]


def densify(count, source, relation, values, dense, acc):
    acc[...] = jnp.zeros_like(acc)

    def add(t, _):
        spot = relation[t] * SRC + source[t]
        acc[spot] = acc[spot] + values[t].astype(F32)
        return 0

    lax.fori_loop(0, count[0], add, 0)
    for r in range(RELS):
        for s in range(SRC):
            dense[r, :, s * TILE : (s + 1) * TILE] = acc[r * SRC + s].astype(BF)


def aggregate(place, dense, feats, after, send, keep, full):
    for r in range(RELS):
        full[:, r * DIN : (r + 1) * DIN] = jnp.dot(dense[r], feats[...], preferred_element_type=F32)
    full[:, RELS * DIN :] = jnp.zeros((TILE, 8 * CHUNK - RELS * DIN), F32)
    core = place[1]
    for z in range(4):
        keep[z] = full[:, pl.ds(pl.multiple_of((2 * z + core) * CHUNK, CHUNK), CHUNK)]
        send[z] = full[:, pl.ds(pl.multiple_of((2 * z + 1 - core) * CHUNK, CHUNK), CHUNK)].astype(BF)


def arrange(sums, own, msgs):
    src = lax.broadcasted_iota(jnp.int32, (CHUNK + TILE, DIN), 0)
    out = lax.broadcasted_iota(jnp.int32, (CHUNK + TILE, DIN), 1)
    swap = jnp.where(out == PER * (src & (NODES - 1)) + (src >> 6), 1.0, 0.0).astype(BF)
    value = jnp.concatenate([sums[...], own[...]], axis=1)
    msgs[...] = jnp.dot(value, swap, preferred_element_type=F32).astype(BF)


def transform(place, msgs, weights, send, keep, part):
    core = place[1]
    part[...] = jnp.dot(msgs[...], weights[...], preferred_element_type=F32)
    for z in range(4):
        keep[z] = part[pl.ds(pl.multiple_of((2 * z + core) * ROWS, ROWS), ROWS)]
        send[z] = part[pl.ds(pl.multiple_of((2 * z + 1 - core) * ROWS, ROWS), ROWS)].astype(BF)


def pair_sum(keep, got, out):
    out[...] = (keep[...] + got[...].astype(F32)).astype(BF)


def finish(got, out):
    total = got[0].astype(F32)
    for i in range(1, 4):
        total = total + got[i].astype(F32)
    out[...] = jnp.maximum(total, 0.0).astype(BF)


def exchange(x, axis):
    return lax.all_to_all(x, axis, split_axis=0, concat_axis=0, tiled=True)


def spread(x, axis):
    return exchange(jnp.broadcast_to(x, (lax.axis_size(axis), *x.shape)), axis)


def partner(x, axis, mask):
    return lax.ppermute(x, axis, [(i, i ^ mask) for i in range(lax.axis_size(axis))])


def on_device(features, bases, coefficients, tile_values, tile_source, tile_relation, tile_count):
    place = jnp.stack([lax.axis_index(a) for a in REL]).astype(jnp.int32)
    padded, copies = call(
        start,
        (shape(BF, ROWS, 8 * TILE), shape(BF, 4, ROWS, DIN + 8 * TILE)),
        [VMEM] * 3,
        [pltpu.VMEM((8, ROWS, TILE), F32)],
    )(features[0], coefficients, jnp.swapaxes(bases, 0, 1))
    gathered = exchange(copies, "zl")
    dense = call(
        densify,
        shape(BF, RELS, TILE, SRC * TILE),
        [SMEM, SMEM, SMEM, VMEM],
        [pltpu.VMEM((RELS * SRC, TILE, TILE), F32)],
        pl.CostEstimate(flops=1 << 20, bytes_accessed=1 << 23, transcendentals=0),
    )(tile_count[0], tile_source[0, 0], tile_relation[0, 0], tile_values[0, 0])
    feats = spread(gathered[:, :, :DIN].reshape(NODES, DIN), YX).reshape(SRC * TILE, DIN)

    parcel = shape(BF, 4, ROWS + 4 * PER, TILE)
    send, keep = call(sort, (parcel, parcel), [SMEM, VMEM, VMEM])(place, padded, gathered)
    block = shape(BF, 2, ROWS + 4 * PER, TILE)
    blocks = shape(BF, 2, 2, ROWS + 4 * PER, TILE)
    send, mine, relay = call(join_cores, (blocks, block, block), [SMEM, VMEM, VMEM])(
        place, keep, partner(send, "core", 1)
    )
    first = partner(send, "zh", 1)
    relay = call(pass_on, blocks, [VMEM] * 2)(relay, first)
    second = partner(relay, "zh", 3)
    own, rows = call(
        join_groups,
        (shape(BF, 8, ROWS, TILE), shape(BF, 4 * PER, DOUT)),
        [SMEM] + [VMEM] * 3,
    )(place, mine, first, second)

    send, keep = call(
        aggregate,
        (shape(BF, 4, TILE, CHUNK), shape(F32, 4, TILE, CHUNK)),
        [SMEM, VMEM, VMEM, ANY],
        [pltpu.VMEM((TILE, 8 * CHUNK), F32)],
    )(place, dense, feats, relay)
    pair = call(pair_sum, shape(BF, 4, TILE, CHUNK), [VMEM] * 2)(keep, partner(send, "core", 1))
    sums = lax.psum_scatter(pair.reshape(4 * TILE, CHUNK), "zh", scatter_dimension=0, tiled=True)
    weights = spread(rows, YX).reshape(NODES * PER, DOUT)
    msgs = call(
        arrange,
        shape(BF, TILE, DIN),
        [VMEM] * 2,
        cost=pl.CostEstimate(flops=WEIGHT, bytes_accessed=1 << 20, transcendentals=0),
    )(sums, own.reshape(TILE, TILE))
    send, keep = call(
        transform,
        (shape(BF, 4, ROWS, DOUT), shape(F32, 4, ROWS, DOUT)),
        [SMEM] + [VMEM] * 2,
        [pltpu.VMEM((TILE, DOUT), F32)],
    )(place, msgs, weights)
    pair = call(pair_sum, shape(BF, 4, ROWS, DOUT), [VMEM] * 2)(keep, partner(send, "core", 1))
    return call(finish, shape(BF, ROWS, DOUT), [VMEM])(exchange(pair, "zh"))[None]


def solution(mesh):
    split = Mesh(mesh.devices.reshape(4, 4, 4, 4, 2), NODE + REL)
    return jax.shard_map(
        on_device,
        mesh=split,
        in_specs=(
            P(REL, NODE, None),
            P(None, NODE, REL),
            P(),
            P(NODE, REL, None, None, None),
            P(NODE, REL, None),
            P(NODE, REL, None),
            P(NODE, REL),
        ),
        out_specs=P(REL, NODE, None),
        check_vma=False,
    )
```

```python
import functools

import jax
import jax.numpy as jnp
from jax import lax
from jax.experimental import pallas as pl
from jax.experimental.pallas import tpu as pltpu
from jax.sharding import Mesh
from jax.sharding import PartitionSpec as P

BF = jnp.bfloat16
F32 = jnp.float32
NODE = ("y", "x", "zl")
REL = ("zh", "core")
YX = ("y", "x")
VMEM = pl.BlockSpec(memory_space=pltpu.VMEM)
ANY = pl.BlockSpec(memory_space=pl.ANY)
HBM = pl.BlockSpec(memory_space=pltpu.HBM)
SMEM = pl.BlockSpec(memory_space=pltpu.SMEM)
PARAMS = pltpu.CompilerParams(vmem_limit_bytes=16 * 1024 * 1024)

RELS = 5
DIN = 768
DOUT = 1024
TILE = 128
SRC = 8
ROWS = 16
NODES = 64
PER = 12
SLOT = 8
SELF = 2
CHUNK = SLOT * NODES
HALF = TILE // 2
PIECE = 256
WEIGHT = 10**11


def call(body, outs, ins, scratch=(), cost=None):
    return pl.pallas_call(
        body,
        cost_estimate=cost,
        out_shape=outs,
        in_specs=ins,
        out_specs=jax.tree.map(lambda _: VMEM, outs),
        scratch_shapes=list(scratch),
        compiler_params=PARAMS,
    )


def shape(kind, *dims):
    return jax.ShapeDtypeStruct(dims, kind)


def start(own_in, coef_in, bases_in, padded, copies, own, coef, bases, rows, sems):
    moves = [
        pltpu.make_async_copy(src, dst, sems.at[i])
        for i, (src, dst) in enumerate(((own_in, own), (coef_in, coef), (bases_in, bases)))
    ]
    for move in moves:
        move.start()
    src = lax.broadcasted_iota(jnp.int32, (DIN, DIN), 0)
    out = lax.broadcasted_iota(jnp.int32, (DIN, DIN), 1)
    swap = jnp.where(src == PER * (out & (NODES - 1)) + (out >> 6), 1.0, 0.0).astype(BF)
    for move in moves:
        move.wait()
    value = jnp.dot(own[...], swap, preferred_element_type=F32).astype(BF)
    padded[:, :DIN] = value
    padded[:, DIN:] = jnp.zeros((ROWS, 8 * TILE - DIN), BF)
    rows[...] = jnp.zeros_like(rows)
    for d in range(PER):
        part = jnp.dot(
            coef[...], bases[d].astype(F32), precision=lax.Precision.HIGHEST, preferred_element_type=F32
        )
        for r in range(RELS):
            j = r * PER + d
            rows[j // SLOT, j % SLOT : j % SLOT + 1] = part[r : r + 1]
        rows[d // SELF, SLOT + d % SELF : SLOT + d % SELF + 1] = part[RELS :]
    for i in range(4):
        copies[i, :, :DIN] = value
        for k in range(8):
            copies[i, :, DIN + k * TILE : DIN + (k + 1) * TILE] = rows[k].astype(BF)


def sort(place, padded, gathered, send, keep):
    core = place[1]

    def fill(ref, z, k):
        ref[z, :ROWS] = padded[:, pl.ds(pl.multiple_of(k * TILE, TILE), TILE)]
        spot = pl.ds(pl.multiple_of(DIN + k * TILE, TILE), TILE)
        rows = [gathered[i, :, spot].astype(F32)[:PER] for i in range(4)]
        ref[z, ROWS:] = jnp.concatenate(rows, axis=0).astype(BF)

    for z in range(4):
        fill(keep, z, 2 * z + core)
        fill(send, z, 2 * z + 1 - core)


def join_cores(place, keep, got, gathered, send, mine, relay, feats):
    feats[...] = gathered[:, :, :DIN].reshape(NODES, DIN)
    zh, core = place[0], place[1]
    for e, ref in ((1, send.at[0]), (2, send.at[1]), (0, mine), (3, relay)):
        z = zh ^ e
        ref[core] = keep[z]
        ref[1 - core] = got[z]


def pass_on(relay, got, send):
    send[0] = relay[...]
    send[1] = got[1]


def join_groups(place, mine, first, second, own, rows):
    for e, ref in ((0, mine), (1, first.at[0]), (3, second.at[0]), (2, second.at[1])):
        z = place[0] ^ e
        for c in range(2):
            g = 2 * z + c
            own[g] = ref[c, :ROWS]
            rows[:, pl.ds(pl.multiple_of(g * TILE, TILE), TILE)] = ref[c, ROWS:]


def densify(count, source, relation, values, dense, acc):
    acc[...] = jnp.zeros_like(acc)

    def add(t, _):
        spot = relation[t] * SRC + source[t]
        acc[spot] = acc[spot] + values[t].astype(F32)
        return 0

    lax.fori_loop(0, count[0], add, 0)
    for r in range(RELS):
        for s in range(SRC):
            dense[r, :, s * TILE : (s + 1) * TILE] = acc[r * SRC + s].astype(BF)
    dense[RELS] = jnp.zeros((TILE, SRC * TILE), BF)


def aggregate(owner, place, dense, feats, after, out):
    core = place[1] ^ owner
    for e in range(4):
        for i in range(2):
            piece = 2 * (2 * (place[0] ^ e) + core) + i
            spot = pl.ds(pl.multiple_of(lax.rem(piece, 3) * PIECE, PIECE), PIECE)
            value = jnp.dot(dense[lax.div(piece, 3)], feats[:, spot], preferred_element_type=F32)
            out[e, :, i * PIECE : (i + 1) * PIECE] = value.astype(out.dtype)


def first_half(keep, got, send_a, send_b, keep_a, keep_b):
    def total(e, rows):
        return keep[e, rows] + got[e, rows].astype(F32)

    a, b = slice(0, HALF), slice(HALF, TILE)
    send_a[0] = total(1, a).astype(BF)
    send_a[1] = total(2, a).astype(BF)
    send_b[0] = total(3, b).astype(BF)
    send_b[1] = total(2, b).astype(BF)
    keep_a[0] = total(0, a)
    keep_a[1] = total(3, a)
    keep_b[0] = total(0, b)
    keep_b[1] = total(1, b)


def second_half(keep_a, keep_b, got_a, got_b, send_a, send_b, hold):
    hold[:HALF] = keep_a[0] + got_a[0].astype(F32)
    hold[HALF:] = keep_b[0] + got_b[0].astype(F32)
    send_a[...] = (keep_a[1] + got_a[1].astype(F32)).astype(BF)
    send_b[...] = (keep_b[1] + got_b[1].astype(F32)).astype(BF)


def transform(place, hold, got_a, got_b, own, weights, send, keep, part):
    core = place[1]
    src = lax.broadcasted_iota(jnp.int32, (CHUNK + TILE, DIN), 0)
    out = lax.broadcasted_iota(jnp.int32, (CHUNK + TILE, DIN), 1)
    swap = jnp.where(out == PER * (src & (NODES - 1)) + (src >> 6), 1.0, 0.0).astype(BF)
    top = (hold[:HALF] + got_a[...].astype(F32)).astype(BF)
    low = (hold[HALF:] + got_b[...].astype(F32)).astype(BF)
    msgs = jnp.concatenate([jnp.concatenate([top, low], axis=0), own[...]], axis=1)
    msgs = jnp.dot(msgs, swap, preferred_element_type=F32).astype(BF)
    part[...] = jnp.dot(msgs, weights[...], preferred_element_type=F32)
    for z in range(4):
        keep[z] = part[pl.ds(pl.multiple_of((2 * z + core) * ROWS, ROWS), ROWS)]
        send[z] = part[pl.ds(pl.multiple_of((2 * z + 1 - core) * ROWS, ROWS), ROWS)].astype(BF)


def pair_sum(keep, got, out):
    out[...] = (keep[...] + got[...].astype(F32)).astype(BF)


def finish(got, out):
    total = got[0].astype(F32)
    for i in range(1, 4):
        total = total + got[i].astype(F32)
    out[...] = jnp.maximum(total, 0.0).astype(BF)


def exchange(x, axis):
    return lax.all_to_all(x, axis, split_axis=0, concat_axis=0, tiled=True)


def spread(x, axis):
    return exchange(jnp.broadcast_to(x, (lax.axis_size(axis), *x.shape)), axis)


def partner(x, axis, mask):
    return lax.ppermute(x, axis, [(i, i ^ mask) for i in range(lax.axis_size(axis))])


def on_device(features, bases, coefficients, tile_values, tile_source, tile_relation, tile_count):
    place = jnp.stack([lax.axis_index(a) for a in REL]).astype(jnp.int32)
    padded, copies = call(
        start,
        (shape(BF, ROWS, 8 * TILE), shape(BF, 4, ROWS, DIN + 8 * TILE)),
        [HBM] * 3,
        [
            pltpu.VMEM((ROWS, DIN), BF),
            pltpu.VMEM((RELS + 1, bases.shape[0]), F32),
            pltpu.VMEM((PER, bases.shape[0], TILE), BF),
            pltpu.VMEM((8, ROWS, TILE), F32),
            pltpu.SemaphoreType.DMA((3,)),
        ],
    )(features[0], coefficients, jnp.swapaxes(bases, 0, 1))
    gathered = exchange(copies, "zl")
    dense = call(
        densify,
        shape(BF, RELS + 1, TILE, SRC * TILE),
        [SMEM, SMEM, SMEM, VMEM],
        [pltpu.VMEM((RELS * SRC, TILE, TILE), F32)],
        pl.CostEstimate(flops=1 << 20, bytes_accessed=1 << 23, transcendentals=0),
    )(tile_count[0], tile_source[0, 0], tile_relation[0, 0], tile_values[0, 0])
    parcel = shape(BF, 4, ROWS + 4 * PER, TILE)
    send, keep = call(sort, (parcel, parcel), [SMEM, VMEM, VMEM])(place, padded, gathered)
    block = shape(BF, 2, ROWS + 4 * PER, TILE)
    blocks = shape(BF, 2, 2, ROWS + 4 * PER, TILE)
    send, mine, relay, feats = call(
        join_cores, (blocks, block, block, shape(BF, NODES, DIN)), [SMEM] + [VMEM] * 3
    )(place, keep, partner(send, "core", 1), gathered)
    feats = spread(feats, YX).reshape(SRC * TILE, DIN)
    first = partner(send, "zh", 1)
    relay = call(pass_on, blocks, [VMEM] * 2)(relay, first)
    second = partner(relay, "zh", 3)
    own, rows = call(
        join_groups,
        (shape(BF, 8, ROWS, TILE), shape(BF, 4 * PER, DOUT)),
        [SMEM] + [VMEM] * 3,
    )(place, mine, first, second)

    send = call(functools.partial(aggregate, 1), shape(BF, 4, TILE, CHUNK), [SMEM, VMEM, VMEM, ANY])(
        place, dense, feats, rows
    )
    keep = call(functools.partial(aggregate, 0), shape(F32, 4, TILE, CHUNK), [SMEM, VMEM, VMEM, ANY])(
        place, dense, feats, send
    )
    two = shape(BF, 2, HALF, CHUNK)
    wide = shape(F32, 2, HALF, CHUNK)
    send_a, send_b, keep_a, keep_b = call(first_half, (two, two, wide, wide), [VMEM] * 2)(
        keep, partner(send, "core", 1)
    )
    one = shape(BF, HALF, CHUNK)
    send_a, send_b, hold = call(
        second_half,
        (one, one, shape(F32, TILE, CHUNK)),
        [VMEM] * 4,
        cost=pl.CostEstimate(flops=WEIGHT, bytes_accessed=1 << 20, transcendentals=0),
    )(keep_a, keep_b, partner(send_a, "zh", 1), partner(send_b, "zh", 3))
    weights = spread(rows, YX).reshape(NODES * PER, DOUT)
    send, keep = call(
        transform,
        (shape(BF, 4, ROWS, DOUT), shape(F32, 4, ROWS, DOUT)),
        [SMEM] + [VMEM] * 5,
        [pltpu.VMEM((TILE, DOUT), F32)],
    )(place, hold, partner(send_a, "zh", 3), partner(send_b, "zh", 1), own.reshape(TILE, TILE), weights)
    pair = call(pair_sum, shape(BF, 4, ROWS, DOUT), [VMEM] * 2)(keep, partner(send, "core", 1))
    return call(finish, shape(BF, ROWS, DOUT), [VMEM])(exchange(pair, "zh"))[None]


def solution(mesh):
    split = Mesh(mesh.devices.reshape(4, 4, 4, 4, 2), NODE + REL)
    return jax.shard_map(
        on_device,
        mesh=split,
        in_specs=(
            P(REL, NODE, None),
            P(None, NODE, REL),
            P(),
            P(NODE, REL, None, None, None),
            P(NODE, REL, None),
            P(NODE, REL, None),
            P(NODE, REL),
        ),
        out_specs=P(REL, NODE, None),
        check_vma=False,
    )
```

```python
import functools

import jax
import jax.numpy as jnp
from jax import lax
from jax.experimental import pallas as pl
from jax.experimental.pallas import tpu as pltpu
from jax.sharding import Mesh
from jax.sharding import PartitionSpec as P

BF = jnp.bfloat16
F32 = jnp.float32
NODE = ("y", "x", "zl")
REL = ("zh", "core")
YX = ("y", "x")
VMEM = pl.BlockSpec(memory_space=pltpu.VMEM)
ANY = pl.BlockSpec(memory_space=pl.ANY)
HBM = pl.BlockSpec(memory_space=pltpu.HBM)
SMEM = pl.BlockSpec(memory_space=pltpu.SMEM)

RELS = 5
DIN = 768
DOUT = 1024
TILE = 128
SRC = 8
ROWS = 16
NODES = 64
PER = 12
SLOT = 8
SELF = 2
CHUNK = SLOT * NODES
QUART = 2 * (SLOT + SELF)
DEPTH = QUART * NODES
WIDE = DOUT // 2
HALF = TILE // 2
PIECE = 256
WEIGHT = 10**11


def call(body, outs, ins, scratch=(), cost=None, limit=16):
    return pl.pallas_call(
        body,
        cost_estimate=cost,
        out_shape=outs,
        in_specs=ins,
        out_specs=jax.tree.map(lambda _: VMEM, outs),
        scratch_shapes=list(scratch),
        compiler_params=pltpu.CompilerParams(vmem_limit_bytes=limit * 1024 * 1024),
    )


def shape(kind, *dims):
    return jax.ShapeDtypeStruct(dims, kind)


def start(own_in, coef_in, bases_in, padded, copies, own, coef, bases, rows, sems):
    moves = [
        pltpu.make_async_copy(src, dst, sems.at[i])
        for i, (src, dst) in enumerate(((own_in, own), (coef_in, coef), (bases_in, bases)))
    ]
    for move in moves:
        move.start()
    src = lax.broadcasted_iota(jnp.int32, (DIN, DIN), 0)
    out = lax.broadcasted_iota(jnp.int32, (DIN, DIN), 1)
    swap = jnp.where(src == PER * (out & (NODES - 1)) + (out >> 6), 1.0, 0.0).astype(BF)
    for move in moves:
        move.wait()
    value = jnp.dot(own[...], swap, preferred_element_type=F32).astype(BF)
    padded[:, :DIN] = value
    padded[:, DIN:] = jnp.zeros((ROWS, 8 * TILE - DIN), BF)
    rows[...] = jnp.zeros_like(rows)
    for d in range(PER):
        part = jnp.dot(
            coef[...], bases[d].astype(F32), precision=lax.Precision.HIGHEST, preferred_element_type=F32
        )
        for r in range(RELS):
            j = r * PER + d
            rows[j // SLOT, j % SLOT : j % SLOT + 1] = part[r : r + 1]
        rows[d // SELF, SLOT + d % SELF : SLOT + d % SELF + 1] = part[RELS :]
    for i in range(4):
        copies[i, :, :DIN] = value
        for k in range(8):
            copies[i, :, DIN + k * TILE : DIN + (k + 1) * TILE] = rows[k].astype(BF)


def sort(place, padded, gathered, send, mine, relay):
    for e, ref in ((1, send.at[0]), (2, send.at[1]), (0, mine), (3, relay)):
        first = (place[0] ^ e) * 2 * TILE
        for i in range(2):
            ref[i * ROWS : (i + 1) * ROWS] = padded[:, pl.ds(pl.multiple_of(first + i * TILE, TILE), TILE)]
        rows = []
        for z in range(4):
            a, b = (
                gathered[z, :, pl.ds(pl.multiple_of(DIN + first + i * TILE, TILE), TILE)].astype(F32)
                for i in range(2)
            )
            rows += [a[:SLOT], b[:SLOT], a[SLOT : SLOT + SELF], b[SLOT : SLOT + SELF]]
        ref[2 * ROWS :] = jnp.concatenate(rows, axis=0).astype(BF)


def pass_on(relay, got, send):
    send[0] = relay[...]
    send[1] = got[1]


def join_groups(place, mine, first, second, own, rows):
    for e, ref in ((0, mine), (1, first.at[0]), (3, second.at[0]), (2, second.at[1])):
        z = place[0] ^ e
        spot = pl.ds(pl.multiple_of(z * ROWS, ROWS), ROWS)
        own[spot, :TILE] = ref[:ROWS]
        own[spot, TILE:] = ref[ROWS : 2 * ROWS]
        rows[:, pl.ds(pl.multiple_of(z * TILE, TILE), TILE)] = ref[2 * ROWS :]


def densify(count, source, relation, values, dense, acc):
    acc[...] = jnp.zeros_like(acc)

    def add(t, _):
        spot = relation[t] * SRC + source[t]
        acc[spot] = acc[spot] + values[t].astype(F32)
        return 0

    lax.fori_loop(0, count[0], add, 0)
    for r in range(RELS):
        for s in range(SRC):
            dense[r, :, s * TILE : (s + 1) * TILE] = acc[r * SRC + s].astype(BF)
    dense[RELS] = jnp.zeros((TILE, SRC * TILE), BF)


def aggregate(owner, place, dense, feats, after, out):
    core = place[1] ^ owner
    for e in range(4):
        for i in range(2):
            piece = 2 * (2 * (place[0] ^ e) + core) + i
            spot = pl.ds(pl.multiple_of(lax.rem(piece, 3) * PIECE, PIECE), PIECE)
            value = jnp.dot(dense[lax.div(piece, 3)], feats[:, spot], preferred_element_type=F32)
            out[e, :, i * PIECE : (i + 1) * PIECE] = value.astype(out.dtype)


def first_half(keep, got, send_a, send_b, keep_a, keep_b):
    def total(e, rows):
        return keep[e, rows] + got[e, rows].astype(F32)

    a, b = slice(0, HALF), slice(HALF, TILE)
    send_a[0] = total(1, a).astype(BF)
    send_a[1] = total(2, a).astype(BF)
    send_b[0] = total(3, b).astype(BF)
    send_b[1] = total(2, b).astype(BF)
    keep_a[0] = total(0, a)
    keep_a[1] = total(3, a)
    keep_b[0] = total(0, b)
    keep_b[1] = total(1, b)


def second_half(keep_a, keep_b, got_a, got_b, send_a, send_b, hold):
    hold[:HALF] = keep_a[0] + got_a[0].astype(F32)
    hold[HALF:] = keep_b[0] + got_b[0].astype(F32)
    send_a[...] = (keep_a[1] + got_a[1].astype(F32)).astype(BF)
    send_b[...] = (keep_b[1] + got_b[1].astype(F32)).astype(BF)


def settle(hold, got_a, got_b, own, msgs):
    msgs[:HALF] = (hold[:HALF] + got_a[...].astype(F32)).astype(BF)
    msgs[HALF:TILE] = (hold[HALF:] + got_b[...].astype(F32)).astype(BF)
    msgs[TILE:, : 2 * TILE] = own[...]
    msgs[TILE:, 2 * TILE :] = jnp.zeros((4 * ROWS, CHUNK - 2 * TILE), BF)


def order(swap):
    src = lax.broadcasted_iota(jnp.int32, (DEPTH, DEPTH), 0)
    out = lax.broadcasted_iota(jnp.int32, (DEPTH, DEPTH), 1)
    swap[...] = jnp.where(out == QUART * (src & (NODES - 1)) + (src >> 6), 1.0, 0.0).astype(BF)


def transform(place, msgs, got, swap, weights, send, full):
    core = place[1]
    for c, ref in ((core, msgs), (1 - core, got)):
        full[:, pl.ds(pl.multiple_of(c * CHUNK, CHUNK), CHUNK)] = ref[:TILE]
        for z in range(4):
            spot = pl.ds(pl.multiple_of((2 * z + c) * ROWS, ROWS), ROWS)
            full[spot, 2 * CHUNK :] = ref[TILE + z * ROWS : TILE + (z + 1) * ROWS, : 2 * TILE]
    value = jnp.dot(full[...], swap[...], preferred_element_type=F32).astype(BF)
    send[...] = jnp.dot(value, weights[...], preferred_element_type=F32).astype(BF)


def finish(place, got, mine, other, total):
    value = got[0].astype(F32)
    for i in range(1, 4):
        value = value + got[i].astype(F32)
    total[...] = jnp.maximum(value, 0.0)
    core = place[1]
    mine[...] = total[pl.ds(pl.multiple_of(core * ROWS, ROWS), ROWS)].astype(BF)
    other[...] = total[pl.ds(pl.multiple_of((1 - core) * ROWS, ROWS), ROWS)].astype(BF)


def place_columns(place, mine, got, out):
    core = place[1]
    for c, ref in ((core, mine), (1 - core, got)):
        for z in range(4):
            spot = pl.ds(pl.multiple_of((2 * z + c) * TILE, TILE), TILE)
            out[:, spot] = ref[:, z * TILE : (z + 1) * TILE]


def exchange(x, axis):
    return lax.all_to_all(x, axis, split_axis=0, concat_axis=0, tiled=True)


def spread(x, axis):
    return exchange(jnp.broadcast_to(x, (lax.axis_size(axis), *x.shape)), axis)


def partner(x, axis, mask):
    return lax.ppermute(x, axis, [(i, i ^ mask) for i in range(lax.axis_size(axis))])


def on_device(features, bases, coefficients, tile_values, tile_source, tile_relation, tile_count):
    place = jnp.stack([lax.axis_index(a) for a in REL]).astype(jnp.int32)
    padded, copies = call(
        start,
        (shape(BF, ROWS, 8 * TILE), shape(BF, 4, ROWS, DIN + 8 * TILE)),
        [HBM] * 3,
        [
            pltpu.VMEM((ROWS, DIN), BF),
            pltpu.VMEM((RELS + 1, bases.shape[0]), F32),
            pltpu.VMEM((PER, bases.shape[0], TILE), BF),
            pltpu.VMEM((8, ROWS, TILE), F32),
            pltpu.SemaphoreType.DMA((3,)),
        ],
        limit=60,
    )(features[0], coefficients, jnp.swapaxes(bases, 0, 1))
    gathered = exchange(copies, "zl")
    dense = call(
        densify,
        shape(BF, RELS + 1, TILE, SRC * TILE),
        [SMEM, SMEM, SMEM, VMEM],
        [pltpu.VMEM((RELS * SRC, TILE, TILE), F32)],
        pl.CostEstimate(flops=1 << 20, bytes_accessed=1 << 23, transcendentals=0),
    )(tile_count[0], tile_source[0, 0], tile_relation[0, 0], tile_values[0, 0])
    feats = spread(gathered[:, :, :DIN].reshape(NODES, DIN), YX).reshape(SRC * TILE, DIN)

    block = shape(BF, 2 * ROWS + 4 * QUART, TILE)
    blocks = shape(BF, 2, 2 * ROWS + 4 * QUART, TILE)
    send, mine, relay = call(sort, (blocks, block, block), [SMEM, VMEM, VMEM])(place, padded, gathered)
    first = partner(send, "zh", 1)
    relay = call(pass_on, blocks, [VMEM] * 2)(relay, first)
    second = partner(relay, "zh", 3)
    own, rows = call(
        join_groups,
        (shape(BF, 4 * ROWS, 2 * TILE), shape(BF, 4 * QUART, WIDE)),
        [SMEM] + [VMEM] * 3,
    )(place, mine, first, second)

    send = call(functools.partial(aggregate, 1), shape(BF, 4, TILE, CHUNK), [SMEM, VMEM, VMEM, ANY])(
        place, dense, feats, rows
    )
    keep = call(functools.partial(aggregate, 0), shape(F32, 4, TILE, CHUNK), [SMEM, VMEM, VMEM, ANY])(
        place, dense, feats, send
    )
    two = shape(BF, 2, HALF, CHUNK)
    wide = shape(F32, 2, HALF, CHUNK)
    send_a, send_b, keep_a, keep_b = call(first_half, (two, two, wide, wide), [VMEM] * 2)(
        keep, partner(send, "core", 1)
    )
    one = shape(BF, HALF, CHUNK)
    send_a, send_b, hold = call(
        second_half,
        (one, one, shape(F32, TILE, CHUNK)),
        [VMEM] * 4,
        cost=pl.CostEstimate(flops=WEIGHT, bytes_accessed=1 << 20, transcendentals=0),
    )(keep_a, keep_b, partner(send_a, "zh", 1), partner(send_b, "zh", 3))
    weights = spread(rows, YX).reshape(DEPTH, WIDE)
    msgs = call(settle, shape(BF, TILE + 4 * ROWS, CHUNK), [VMEM] * 4)(
        hold, partner(send_a, "zh", 3), partner(send_b, "zh", 1), own
    )
    swap = call(order, shape(BF, DEPTH, DEPTH), [])()
    send = call(
        transform,
        shape(BF, TILE, WIDE),
        [SMEM] + [VMEM] * 4,
        [pltpu.VMEM((TILE, DEPTH), BF)],
    )(place, msgs, partner(msgs, "core", 1), swap, weights)
    half = shape(BF, ROWS, WIDE)
    mine, other = call(finish, (half, half), [SMEM, VMEM], [pltpu.VMEM((2 * ROWS, WIDE), F32)])(
        place, exchange(send.reshape(4, 2 * ROWS, WIDE), "zh")
    )
    out = call(place_columns, shape(BF, ROWS, DOUT), [SMEM, VMEM, VMEM])(
        place, mine, partner(other, "core", 1)
    )
    return out[None]


def solution(mesh):
    split = Mesh(mesh.devices.reshape(4, 4, 4, 4, 2), NODE + REL)
    return jax.shard_map(
        on_device,
        mesh=split,
        in_specs=(
            P(REL, NODE, None),
            P(None, NODE, REL),
            P(),
            P(NODE, REL, None, None, None),
            P(NODE, REL, None),
            P(NODE, REL, None),
            P(NODE, REL),
        ),
        out_specs=P(REL, NODE, None),
        check_vma=False,
    )
```

```python
import functools

import jax
import jax.numpy as jnp
from jax import lax
from jax.experimental import pallas as pl
from jax.experimental.pallas import tpu as pltpu
from jax.sharding import Mesh
from jax.sharding import PartitionSpec as P

BF = jnp.bfloat16
F32 = jnp.float32
NODE = ("y", "x", "zl")
REL = ("zh", "core")
YX = ("y", "x")
VMEM = pl.BlockSpec(memory_space=pltpu.VMEM)
ANY = pl.BlockSpec(memory_space=pl.ANY)
HBM = pl.BlockSpec(memory_space=pltpu.HBM)
SMEM = pl.BlockSpec(memory_space=pltpu.SMEM)

RELS = 5
DIN = 768
DOUT = 1024
TILE = 128
SRC = 8
ROWS = 16
NODES = 64
PER = 12
SLOT = 8
SELF = 2
CHUNK = SLOT * NODES
QUART = 2 * (SLOT + SELF)
DEPTH = QUART * NODES
WIDE = DOUT // 2
PIECE = 256
WEIGHT = 10**11


def call(body, outs, ins, scratch=(), cost=None, limit=16):
    return pl.pallas_call(
        body,
        cost_estimate=cost,
        out_shape=outs,
        in_specs=ins,
        out_specs=jax.tree.map(lambda _: VMEM, outs),
        scratch_shapes=list(scratch),
        compiler_params=pltpu.CompilerParams(vmem_limit_bytes=limit * 1024 * 1024),
    )


def shape(kind, *dims):
    return jax.ShapeDtypeStruct(dims, kind)


def start(own_in, coef_in, bases_in, padded, copies, own, coef, bases, rows, sems):
    moves = [
        pltpu.make_async_copy(src, dst, sems.at[i])
        for i, (src, dst) in enumerate(((own_in, own), (coef_in, coef), (bases_in, bases)))
    ]
    for move in moves:
        move.start()
    src = lax.broadcasted_iota(jnp.int32, (DIN, DIN), 0)
    out = lax.broadcasted_iota(jnp.int32, (DIN, DIN), 1)
    swap = jnp.where(src == PER * (out & (NODES - 1)) + (out >> 6), 1.0, 0.0).astype(BF)
    for move in moves:
        move.wait()
    value = jnp.dot(own[...], swap, preferred_element_type=F32).astype(BF)
    padded[:, :DIN] = value
    padded[:, DIN:] = jnp.zeros((ROWS, 8 * TILE - DIN), BF)
    rows[...] = jnp.zeros_like(rows)
    for d in range(PER):
        part = jnp.dot(
            coef[...], bases[d].astype(F32), precision=lax.Precision.HIGHEST, preferred_element_type=F32
        )
        for r in range(RELS):
            j = r * PER + d
            rows[j // SLOT, j % SLOT : j % SLOT + 1] = part[r : r + 1]
        rows[d // SELF, SLOT + d % SELF : SLOT + d % SELF + 1] = part[RELS :]
    for i in range(4):
        copies[i, :, :DIN] = value
        for k in range(8):
            copies[i, :, DIN + k * TILE : DIN + (k + 1) * TILE] = rows[k].astype(BF)


def ranks(zh, core):
    one = 1 + 2 * core
    return zh, zh ^ one, zh ^ 2, zh ^ (4 - one)


def sort(place, padded, gathered, send, mine, relay):
    here, near, far, last = ranks(place[0], place[1])
    for z, ref in ((near, send.at[0]), (far, send.at[1]), (here, mine), (last, relay)):
        first = z * 2 * TILE
        for i in range(2):
            ref[i * ROWS : (i + 1) * ROWS] = padded[:, pl.ds(pl.multiple_of(first + i * TILE, TILE), TILE)]
        rows = []
        for k in range(4):
            a, b = (
                gathered[k, :, pl.ds(pl.multiple_of(DIN + first + i * TILE, TILE), TILE)].astype(F32)
                for i in range(2)
            )
            rows += [a[:SLOT], b[:SLOT], a[SLOT : SLOT + SELF], b[SLOT : SLOT + SELF]]
        ref[2 * ROWS :] = jnp.concatenate(rows, axis=0).astype(BF)


def pass_on(relay, got, send):
    send[0] = relay[...]
    send[1] = got[1]


def join_groups(place, mine, first, second, own, rows):
    here, near, far, last = ranks(place[0], place[1])
    for z, ref in ((here, mine), (near, first.at[0]), (last, second.at[0]), (far, second.at[1])):
        spot = pl.ds(pl.multiple_of(z * ROWS, ROWS), ROWS)
        own[spot, :TILE] = ref[:ROWS]
        own[spot, TILE:] = ref[ROWS : 2 * ROWS]
        rows[:, pl.ds(pl.multiple_of(z * TILE, TILE), TILE)] = ref[2 * ROWS :]


def densify(count, source, relation, values, dense, acc):
    acc[...] = jnp.zeros_like(acc)

    def add(t, _):
        spot = relation[t] * SRC + source[t]
        acc[spot] = acc[spot] + values[t].astype(F32)
        return 0

    lax.fori_loop(0, count[0], add, 0)
    for r in range(RELS):
        for s in range(SRC):
            dense[r, :, s * TILE : (s + 1) * TILE] = acc[r * SRC + s].astype(BF)
    dense[RELS] = jnp.zeros((TILE, SRC * TILE), BF)


def aggregate(owner, place, dense, feats, after, out):
    core = place[1] ^ owner
    for e, z in enumerate(ranks(place[0], core)):
        for i in range(2):
            piece = 2 * (2 * z + core) + i
            spot = pl.ds(pl.multiple_of(lax.rem(piece, 3) * PIECE, PIECE), PIECE)
            value = jnp.dot(dense[lax.div(piece, 3)], feats[:, spot], preferred_element_type=F32)
            out[e, :, i * PIECE : (i + 1) * PIECE] = value.astype(out.dtype)


def first_half(keep, got, send, rest):
    def total(e):
        return keep[e] + got[e].astype(F32)

    send[0] = total(1).astype(BF)
    send[1] = total(2).astype(BF)
    rest[0] = total(0)
    rest[1] = total(3)


def second_half(rest, got, send, hold):
    hold[...] = rest[0] + got[0].astype(F32)
    send[...] = (rest[1] + got[1].astype(F32)).astype(BF)


def settle(hold, got, own, msgs):
    msgs[:TILE] = (hold[...] + got[...].astype(F32)).astype(BF)
    msgs[TILE:, : 2 * TILE] = own[...]
    msgs[TILE:, 2 * TILE :] = jnp.zeros((4 * ROWS, CHUNK - 2 * TILE), BF)


def order(swap):
    src = lax.broadcasted_iota(jnp.int32, (DEPTH, DEPTH), 0)
    out = lax.broadcasted_iota(jnp.int32, (DEPTH, DEPTH), 1)
    swap[...] = jnp.where(out == QUART * (src & (NODES - 1)) + (src >> 6), 1.0, 0.0).astype(BF)


def transform(place, msgs, got, swap, weights, send, full):
    core = place[1]
    for c, ref in ((core, msgs), (1 - core, got)):
        full[:, pl.ds(pl.multiple_of(c * CHUNK, CHUNK), CHUNK)] = ref[:TILE]
        for z in range(4):
            spot = pl.ds(pl.multiple_of((2 * z + c) * ROWS, ROWS), ROWS)
            full[spot, 2 * CHUNK :] = ref[TILE + z * ROWS : TILE + (z + 1) * ROWS, : 2 * TILE]
    value = jnp.dot(full[...], swap[...], preferred_element_type=F32).astype(BF)
    send[...] = jnp.dot(value, weights[...], preferred_element_type=F32).astype(BF)


def finish(place, got, mine, other, total):
    value = got[0].astype(F32)
    for i in range(1, 4):
        value = value + got[i].astype(F32)
    total[...] = jnp.maximum(value, 0.0)
    core = place[1]
    mine[...] = total[pl.ds(pl.multiple_of(core * ROWS, ROWS), ROWS)].astype(BF)
    other[...] = total[pl.ds(pl.multiple_of((1 - core) * ROWS, ROWS), ROWS)].astype(BF)


def place_columns(place, mine, got, out):
    core = place[1]
    for c, ref in ((core, mine), (1 - core, got)):
        for z in range(4):
            spot = pl.ds(pl.multiple_of((2 * z + c) * TILE, TILE), TILE)
            out[:, spot] = ref[:, z * TILE : (z + 1) * TILE]


def exchange(x, axis):
    return lax.all_to_all(x, axis, split_axis=0, concat_axis=0, tiled=True)


def spread(x, axis):
    return exchange(jnp.broadcast_to(x, (lax.axis_size(axis), *x.shape)), axis)


def partner(x, step):
    def goal(zh, core):
        return (zh, 1 - core) if step == 0 else (ranks(zh, core)[2 * step - 1], core)

    pairs = [(2 * z + c, goal(z, c)) for z in range(4) for c in range(2)]
    return lax.ppermute(x, REL, [(i, 2 * z + c) for i, (z, c) in pairs])


def on_device(features, bases, coefficients, tile_values, tile_source, tile_relation, tile_count):
    place = jnp.stack([lax.axis_index(a) for a in REL]).astype(jnp.int32)
    padded, copies = call(
        start,
        (shape(BF, ROWS, 8 * TILE), shape(BF, 4, ROWS, DIN + 8 * TILE)),
        [HBM] * 3,
        [
            pltpu.VMEM((ROWS, DIN), BF),
            pltpu.VMEM((RELS + 1, bases.shape[0]), F32),
            pltpu.VMEM((PER, bases.shape[0], TILE), BF),
            pltpu.VMEM((8, ROWS, TILE), F32),
            pltpu.SemaphoreType.DMA((3,)),
        ],
        limit=60,
    )(features[0], coefficients, jnp.swapaxes(bases, 0, 1))
    gathered = exchange(copies, "zl")
    dense = call(
        densify,
        shape(BF, RELS + 1, TILE, SRC * TILE),
        [SMEM, SMEM, SMEM, VMEM],
        [pltpu.VMEM((RELS * SRC, TILE, TILE), F32)],
        pl.CostEstimate(flops=1 << 20, bytes_accessed=1 << 23, transcendentals=0),
    )(tile_count[0], tile_source[0, 0], tile_relation[0, 0], tile_values[0, 0])
    feats = spread(gathered[:, :, :DIN].reshape(NODES, DIN), YX).reshape(SRC * TILE, DIN)

    block = shape(BF, 2 * ROWS + 4 * QUART, TILE)
    blocks = shape(BF, 2, 2 * ROWS + 4 * QUART, TILE)
    send, mine, relay = call(sort, (blocks, block, block), [SMEM, VMEM, VMEM])(place, padded, gathered)
    first = partner(send, 1)
    relay = call(pass_on, blocks, [VMEM] * 2)(relay, first)
    second = partner(relay, 2)
    own, rows = call(
        join_groups,
        (shape(BF, 4 * ROWS, 2 * TILE), shape(BF, 4 * QUART, WIDE)),
        [SMEM] + [VMEM] * 3,
    )(place, mine, first, second)

    send = call(functools.partial(aggregate, 1), shape(BF, 4, TILE, CHUNK), [SMEM, VMEM, VMEM, ANY])(
        place, dense, feats, rows
    )
    keep = call(functools.partial(aggregate, 0), shape(F32, 4, TILE, CHUNK), [SMEM, VMEM, VMEM, ANY])(
        place, dense, feats, send
    )
    two = shape(BF, 2, TILE, CHUNK)
    send, rest = call(first_half, (two, shape(F32, 2, TILE, CHUNK)), [VMEM] * 2)(keep, partner(send, 0))
    send, hold = call(
        second_half,
        (shape(BF, TILE, CHUNK), shape(F32, TILE, CHUNK)),
        [VMEM] * 2,
        cost=pl.CostEstimate(flops=WEIGHT, bytes_accessed=1 << 20, transcendentals=0),
    )(rest, partner(send, 1))
    weights = spread(rows, YX).reshape(DEPTH, WIDE)
    msgs = call(settle, shape(BF, TILE + 4 * ROWS, CHUNK), [VMEM] * 3)(hold, partner(send, 2), own)
    swap = call(order, shape(BF, DEPTH, DEPTH), [])()
    send = call(
        transform,
        shape(BF, TILE, WIDE),
        [SMEM] + [VMEM] * 4,
        [pltpu.VMEM((TILE, DEPTH), BF)],
    )(place, msgs, partner(msgs, 0), swap, weights)
    half = shape(BF, ROWS, WIDE)
    mine, other = call(finish, (half, half), [SMEM, VMEM], [pltpu.VMEM((2 * ROWS, WIDE), F32)])(
        place, exchange(send.reshape(4, 2 * ROWS, WIDE), "zh")
    )
    out = call(place_columns, shape(BF, ROWS, DOUT), [SMEM, VMEM, VMEM])(
        place, mine, partner(other, 0)
    )
    return out[None]


def solution(mesh):
    split = Mesh(mesh.devices.reshape(4, 4, 4, 4, 2), NODE + REL)
    return jax.shard_map(
        on_device,
        mesh=split,
        in_specs=(
            P(REL, NODE, None),
            P(None, NODE, REL),
            P(),
            P(NODE, REL, None, None, None),
            P(NODE, REL, None),
            P(NODE, REL, None),
            P(NODE, REL),
        ),
        out_specs=P(REL, NODE, None),
        check_vma=False,
    )
```

```python
import functools

import jax
import jax.numpy as jnp
from jax import lax
from jax.experimental import pallas as pl
from jax.experimental.pallas import tpu as pltpu
from jax.sharding import Mesh
from jax.sharding import PartitionSpec as P

BF = jnp.bfloat16
F32 = jnp.float32
NODE = ("y", "x", "zl")
REL = ("zh", "core")
YX = ("y", "x")
VMEM = pl.BlockSpec(memory_space=pltpu.VMEM)
ANY = pl.BlockSpec(memory_space=pl.ANY)
HBM = pl.BlockSpec(memory_space=pltpu.HBM)
SMEM = pl.BlockSpec(memory_space=pltpu.SMEM)

RELS = 5
DIN = 768
DOUT = 1024
TILE = 128
SRC = 8
ROWS = 16
NODES = 64
PER = 12
SLOT = 8
SELF = 2
CHUNK = SLOT * NODES
QUART = 2 * (SLOT + SELF)
DEPTH = QUART * NODES
WIDE = DOUT // 2
PIECE = 256
WEIGHT = 10**11


def call(body, outs, ins, scratch=(), cost=None, limit=16):
    return pl.pallas_call(
        body,
        cost_estimate=cost,
        out_shape=outs,
        in_specs=ins,
        out_specs=jax.tree.map(lambda _: VMEM, outs),
        scratch_shapes=list(scratch),
        compiler_params=pltpu.CompilerParams(vmem_limit_bytes=limit * 1024 * 1024),
    )


def shape(kind, *dims):
    return jax.ShapeDtypeStruct(dims, kind)


def start(own_in, coef_in, bases_in, padded, copies, own, coef, bases, rows, sems):
    moves = [
        pltpu.make_async_copy(src, dst, sems.at[i])
        for i, (src, dst) in enumerate(((own_in, own), (coef_in, coef), (bases_in, bases)))
    ]
    for move in moves:
        move.start()
    src = lax.broadcasted_iota(jnp.int32, (DIN, DIN), 0)
    out = lax.broadcasted_iota(jnp.int32, (DIN, DIN), 1)
    swap = jnp.where(src == PER * (out & (NODES - 1)) + (out >> 6), 1.0, 0.0).astype(BF)
    for move in moves:
        move.wait()
    value = jnp.dot(own[...], swap, preferred_element_type=F32).astype(BF)
    padded[:, :DIN] = value
    padded[:, DIN:] = jnp.zeros((ROWS, 8 * TILE - DIN), BF)
    rows[...] = jnp.zeros_like(rows)
    for d in range(PER):
        part = jnp.dot(
            coef[...], bases[d].astype(F32), precision=lax.Precision.HIGHEST, preferred_element_type=F32
        )
        for r in range(RELS):
            j = r * PER + d
            rows[j // SLOT, j % SLOT : j % SLOT + 1] = part[r : r + 1]
        rows[d // SELF, SLOT + d % SELF : SLOT + d % SELF + 1] = part[RELS :]
    for i in range(4):
        copies[i, :, :DIN] = value
        for k in range(8):
            copies[i, :, DIN + k * TILE : DIN + (k + 1) * TILE] = rows[k].astype(BF)


def ranks(zh, core):
    one = 1 + 2 * core
    return zh, zh ^ one, zh ^ 2, zh ^ (4 - one)


def sort(place, padded, gathered, send, mine, relay):
    here, near, far, last = ranks(place[0], place[1])
    for z, ref in ((near, send.at[0]), (far, send.at[1]), (here, mine), (last, relay)):
        first = z * 2 * TILE
        for i in range(2):
            ref[i * ROWS : (i + 1) * ROWS] = padded[:, pl.ds(pl.multiple_of(first + i * TILE, TILE), TILE)]
        rows = []
        for k in range(4):
            a, b = (
                gathered[k, :, pl.ds(pl.multiple_of(DIN + first + i * TILE, TILE), TILE)].astype(F32)
                for i in range(2)
            )
            rows += [a[:SLOT], b[:SLOT], a[SLOT : SLOT + SELF], b[SLOT : SLOT + SELF]]
        ref[2 * ROWS :] = jnp.concatenate(rows, axis=0).astype(BF)


def pass_on(relay, got, send):
    send[0] = relay[...]
    send[1] = got[1]


def join_groups(place, mine, first, second, own, rows):
    here, near, far, last = ranks(place[0], place[1])
    for z, ref in ((here, mine), (near, first.at[0]), (last, second.at[0]), (far, second.at[1])):
        spot = pl.ds(pl.multiple_of(z * ROWS, ROWS), ROWS)
        own[spot, :TILE] = ref[:ROWS]
        own[spot, TILE:] = ref[ROWS : 2 * ROWS]
        rows[:, pl.ds(pl.multiple_of(z * TILE, TILE), TILE)] = ref[2 * ROWS :]


def densify(count, source, relation, values, dense, acc):
    acc[...] = jnp.zeros_like(acc)

    def add(t, _):
        spot = relation[t] * SRC + source[t]
        acc[spot] = acc[spot] + values[t].astype(F32)
        return 0

    lax.fori_loop(0, count[0], add, 0)
    for r in range(RELS):
        for s in range(SRC):
            dense[r, :, s * TILE : (s + 1) * TILE] = acc[r * SRC + s].astype(BF)
    dense[RELS] = jnp.zeros((TILE, SRC * TILE), BF)


def aggregate(owner, place, dense, feats, after, out):
    core = place[1] ^ owner
    for e, z in enumerate(ranks(place[0], core)):
        for i in range(2):
            piece = 2 * (2 * z + core) + i
            spot = pl.ds(pl.multiple_of(lax.rem(piece, 3) * PIECE, PIECE), PIECE)
            value = jnp.dot(dense[lax.div(piece, 3)], feats[:, spot], preferred_element_type=F32)
            out[e, :, i * PIECE : (i + 1) * PIECE] = value.astype(out.dtype)


def first_half(keep, got, send, rest):
    def total(e):
        return keep[e] + got[e].astype(F32)

    send[0] = total(1).astype(BF)
    send[1] = total(2).astype(BF)
    rest[0] = total(0)
    rest[1] = total(3)


def second_half(rest, got, send, hold):
    hold[...] = rest[0] + got[0].astype(F32)
    send[...] = (rest[1] + got[1].astype(F32)).astype(BF)


def settle(hold, got, own, msgs):
    msgs[:TILE] = (hold[...] + got[...].astype(F32)).astype(BF)
    msgs[TILE:, : 2 * TILE] = own[...]
    msgs[TILE:, 2 * TILE :] = jnp.zeros((4 * ROWS, CHUNK - 2 * TILE), BF)


def order(swap):
    src = lax.broadcasted_iota(jnp.int32, (DEPTH, DEPTH), 0)
    out = lax.broadcasted_iota(jnp.int32, (DEPTH, DEPTH), 1)
    swap[...] = jnp.where(out == QUART * (src & (NODES - 1)) + (src >> 6), 1.0, 0.0).astype(BF)


def transform(place, msgs, got, swap, weights, send, rest, full, part):
    core = place[1]
    for c, ref in ((core, msgs), (1 - core, got)):
        full[:, pl.ds(pl.multiple_of(c * CHUNK, CHUNK), CHUNK)] = ref[:TILE]
        for z in range(4):
            spot = pl.ds(pl.multiple_of((2 * z + c) * ROWS, ROWS), ROWS)
            full[spot, 2 * CHUNK :] = ref[TILE + z * ROWS : TILE + (z + 1) * ROWS, : 2 * TILE]
    value = jnp.dot(full[...], swap[...], preferred_element_type=F32).astype(BF)
    part[...] = jnp.dot(value, weights[...], preferred_element_type=F32)
    here, near, far, last = ranks(place[0], place[1])
    for i, z in enumerate((near, far, here, last)):
        rows = part[pl.ds(pl.multiple_of(z * 2 * ROWS, 2 * ROWS), 2 * ROWS)]
        if i < 2:
            send[i] = rows.astype(BF)
        else:
            rest[i - 2] = rows


def finish(place, hold, got, mine, other, total):
    value = hold[...] + got[...].astype(F32)
    total[...] = jnp.maximum(value, 0.0)
    core = place[1]
    mine[...] = total[pl.ds(pl.multiple_of(core * ROWS, ROWS), ROWS)].astype(BF)
    other[...] = total[pl.ds(pl.multiple_of((1 - core) * ROWS, ROWS), ROWS)].astype(BF)


def place_columns(place, mine, got, out):
    core = place[1]
    for c, ref in ((core, mine), (1 - core, got)):
        for z in range(4):
            spot = pl.ds(pl.multiple_of((2 * z + c) * TILE, TILE), TILE)
            out[:, spot] = ref[:, z * TILE : (z + 1) * TILE]


def exchange(x, axis):
    return lax.all_to_all(x, axis, split_axis=0, concat_axis=0, tiled=True)


def spread(x, axis):
    return exchange(jnp.broadcast_to(x, (lax.axis_size(axis), *x.shape)), axis)


def partner(x, step):
    def goal(zh, core):
        return (zh, 1 - core) if step == 0 else (ranks(zh, core)[2 * step - 1], core)

    pairs = [(2 * z + c, goal(z, c)) for z in range(4) for c in range(2)]
    return lax.ppermute(x, REL, [(i, 2 * z + c) for i, (z, c) in pairs])


def on_device(features, bases, coefficients, tile_values, tile_source, tile_relation, tile_count):
    place = jnp.stack([lax.axis_index(a) for a in REL]).astype(jnp.int32)
    padded, copies = call(
        start,
        (shape(BF, ROWS, 8 * TILE), shape(BF, 4, ROWS, DIN + 8 * TILE)),
        [HBM] * 3,
        [
            pltpu.VMEM((ROWS, DIN), BF),
            pltpu.VMEM((RELS + 1, bases.shape[0]), F32),
            pltpu.VMEM((PER, bases.shape[0], TILE), BF),
            pltpu.VMEM((8, ROWS, TILE), F32),
            pltpu.SemaphoreType.DMA((3,)),
        ],
        limit=60,
    )(features[0], coefficients, jnp.swapaxes(bases, 0, 1))
    gathered = exchange(copies, "zl")
    dense = call(
        densify,
        shape(BF, RELS + 1, TILE, SRC * TILE),
        [SMEM, SMEM, SMEM, VMEM],
        [pltpu.VMEM((RELS * SRC, TILE, TILE), F32)],
        pl.CostEstimate(flops=1 << 20, bytes_accessed=1 << 23, transcendentals=0),
    )(tile_count[0], tile_source[0, 0], tile_relation[0, 0], tile_values[0, 0])
    feats = spread(gathered[:, :, :DIN].reshape(NODES, DIN), YX).reshape(SRC * TILE, DIN)

    block = shape(BF, 2 * ROWS + 4 * QUART, TILE)
    blocks = shape(BF, 2, 2 * ROWS + 4 * QUART, TILE)
    send, mine, relay = call(sort, (blocks, block, block), [SMEM, VMEM, VMEM])(place, padded, gathered)
    first = partner(send, 1)
    relay = call(pass_on, blocks, [VMEM] * 2)(relay, first)
    second = partner(relay, 2)
    own, rows = call(
        join_groups,
        (shape(BF, 4 * ROWS, 2 * TILE), shape(BF, 4 * QUART, WIDE)),
        [SMEM] + [VMEM] * 3,
    )(place, mine, first, second)

    send = call(functools.partial(aggregate, 1), shape(BF, 4, TILE, CHUNK), [SMEM, VMEM, VMEM, ANY])(
        place, dense, feats, rows
    )
    keep = call(functools.partial(aggregate, 0), shape(F32, 4, TILE, CHUNK), [SMEM, VMEM, VMEM, ANY])(
        place, dense, feats, send
    )
    two = shape(BF, 2, TILE, CHUNK)
    send, rest = call(first_half, (two, shape(F32, 2, TILE, CHUNK)), [VMEM] * 2)(keep, partner(send, 0))
    send, hold = call(
        second_half,
        (shape(BF, TILE, CHUNK), shape(F32, TILE, CHUNK)),
        [VMEM] * 2,
        cost=pl.CostEstimate(flops=WEIGHT, bytes_accessed=1 << 20, transcendentals=0),
    )(rest, partner(send, 1))
    weights = spread(rows, YX).reshape(DEPTH, WIDE)
    msgs = call(settle, shape(BF, TILE + 4 * ROWS, CHUNK), [VMEM] * 3)(hold, partner(send, 2), own)
    swap = call(order, shape(BF, DEPTH, DEPTH), [])()
    pair = shape(BF, 2, 2 * ROWS, WIDE)
    send, rest = call(
        transform,
        (pair, shape(F32, 2, 2 * ROWS, WIDE)),
        [SMEM] + [VMEM] * 4,
        [pltpu.VMEM((TILE, DEPTH), BF), pltpu.VMEM((TILE, WIDE), F32)],
    )(place, msgs, partner(msgs, 0), swap, weights)
    send, hold = call(
        second_half, (shape(BF, 2 * ROWS, WIDE), shape(F32, 2 * ROWS, WIDE)), [VMEM] * 2
    )(rest, partner(send, 1))
    half = shape(BF, ROWS, WIDE)
    mine, other = call(finish, (half, half), [SMEM, VMEM, VMEM], [pltpu.VMEM((2 * ROWS, WIDE), F32)])(
        place, hold, partner(send, 2)
    )
    out = call(place_columns, shape(BF, ROWS, DOUT), [SMEM, VMEM, VMEM])(
        place, mine, partner(other, 0)
    )
    return out[None]


def solution(mesh):
    split = Mesh(mesh.devices.reshape(4, 4, 4, 4, 2), NODE + REL)
    return jax.shard_map(
        on_device,
        mesh=split,
        in_specs=(
            P(REL, NODE, None),
            P(None, NODE, REL),
            P(),
            P(NODE, REL, None, None, None),
            P(NODE, REL, None),
            P(NODE, REL, None),
            P(NODE, REL),
        ),
        out_specs=P(REL, NODE, None),
        check_vma=False,
    )
```

```python
import functools

import jax
import jax.numpy as jnp
from jax import lax
from jax.experimental import pallas as pl
from jax.experimental.pallas import tpu as pltpu
from jax.sharding import Mesh
from jax.sharding import PartitionSpec as P

BF = jnp.bfloat16
F32 = jnp.float32
NODE = ("y", "x", "zl")
REL = ("zh", "core")
YX = ("y", "x")
VMEM = pl.BlockSpec(memory_space=pltpu.VMEM)
ANY = pl.BlockSpec(memory_space=pl.ANY)
HBM = pl.BlockSpec(memory_space=pltpu.HBM)
SMEM = pl.BlockSpec(memory_space=pltpu.SMEM)

RELS = 5
DIN = 768
DOUT = 1024
TILE = 128
SRC = 8
ROWS = 16
NODES = 64
PER = 12
SLOT = 8
SELF = 2
CHUNK = SLOT * NODES
QUART = 2 * (SLOT + SELF)
PARTS = 5
WIDE = DOUT // 2
PIECE = 256
WEIGHT = 10**11


def call(body, outs, ins, scratch=(), cost=None, limit=16):
    return pl.pallas_call(
        body,
        cost_estimate=cost,
        out_shape=outs,
        in_specs=ins,
        out_specs=jax.tree.map(lambda _: VMEM, outs),
        scratch_shapes=list(scratch),
        compiler_params=pltpu.CompilerParams(vmem_limit_bytes=limit * 1024 * 1024),
    )


def shape(kind, *dims):
    return jax.ShapeDtypeStruct(dims, kind)


def start(own_in, coef_in, bases_in, padded, copies, own, coef, bases, rows, sems):
    moves = [
        pltpu.make_async_copy(src, dst, sems.at[i])
        for i, (src, dst) in enumerate(((own_in, own), (coef_in, coef), (bases_in, bases)))
    ]
    for move in moves:
        move.start()
    src = lax.broadcasted_iota(jnp.int32, (DIN, DIN), 0)
    out = lax.broadcasted_iota(jnp.int32, (DIN, DIN), 1)
    goal = PER * ((out & (PIECE - 1)) >> 2) + 4 * (out >> 8) + (out & 3)
    swap = jnp.where(src == goal, 1.0, 0.0).astype(BF)
    rows[...] = jnp.zeros_like(rows)
    for move in moves:
        move.wait()
    value = jnp.dot(own[...], swap, preferred_element_type=F32).astype(BF)
    padded[:, :DIN] = value
    padded[:, DIN:] = jnp.zeros((ROWS, 8 * TILE - DIN), BF)
    for d in range(PER):
        part = jnp.dot(
            coef[...], bases[d].astype(F32), precision=lax.Precision.HIGHEST, preferred_element_type=F32
        )
        for r in range(RELS):
            piece = 3 * r + d // 4
            spot = piece // 4 * 4 + d % 4
            rows[piece % 4, spot : spot + 1] = part[r : r + 1]
        rows[PARTS - 1, d : d + 1] = part[RELS:]
    for i in range(4):
        copies[i, :, :DIN] = value
        for k in range(PARTS):
            copies[i, :, DIN + k * TILE : DIN + (k + 1) * TILE] = rows[k].astype(BF)


def ranks(zh, core):
    one = 1 + 2 * core
    return zh, zh ^ one, zh ^ 2, zh ^ (4 - one)


def sort(place, padded, gathered, send, mine, relay, table):
    wide = gathered[:, :, DIN:].astype(F32)
    for z in range(4):
        for i in range(PARTS):
            rows = [wide[k, 4 * z : 4 * z + 4, i * TILE : (i + 1) * TILE] for k in range(4)]
            table[z, i * ROWS : (i + 1) * ROWS] = jnp.concatenate(rows, axis=0).astype(BF)
    here, near, far, last = ranks(place[0], place[1])
    for z, ref in ((near, send.at[0]), (far, send.at[1]), (here, mine), (last, relay)):
        for i in range(2):
            spot = pl.ds(pl.multiple_of(z * PIECE + i * TILE, TILE), TILE)
            ref[i * ROWS : (i + 1) * ROWS] = padded[:, spot]
        ref[2 * ROWS :] = table[z]


def pass_on(after, relay, got, send):
    send[0] = relay[...]
    send[1] = got[1]


def join_groups(place, mine, first, second, own, rows):
    here, near, far, last = ranks(place[0], place[1])
    for z, ref in ((here, mine), (near, first.at[0]), (last, second.at[0]), (far, second.at[1])):
        spot = pl.ds(pl.multiple_of(z * ROWS, ROWS), ROWS)
        own[spot, :TILE] = ref[:ROWS]
        own[spot, TILE:] = ref[ROWS : 2 * ROWS]
        rows[:, pl.ds(pl.multiple_of(z * TILE, TILE), TILE)] = ref[2 * ROWS :]


def densify(count, source, relation, values, dense, acc):
    acc[...] = jnp.zeros_like(acc)

    def add(t, _):
        spot = relation[t] * SRC + source[t]
        acc[spot] = acc[spot] + values[t].astype(F32)
        return 0

    lax.fori_loop(0, count[0], add, 0)
    for r in range(RELS):
        for s in range(SRC):
            dense[r, :, s * TILE : (s + 1) * TILE] = acc[r * SRC + s].astype(BF)
    dense[RELS] = jnp.zeros((TILE, SRC * TILE), BF)


def aggregate(owner, place, dense, feats, after, out):
    core = place[1] ^ owner
    for e, z in enumerate(ranks(place[0], core)):
        for i in range(2):
            piece = 2 * (2 * z + core) + i
            spot = pl.ds(pl.multiple_of(lax.rem(piece, 3) * PIECE, PIECE), PIECE)
            value = jnp.dot(dense[lax.div(piece, 3)], feats[:, spot], preferred_element_type=F32)
            out[e, :, i * PIECE : (i + 1) * PIECE] = value.astype(out.dtype)


def first_half(keep, got, send, rest):
    def total(e):
        return keep[e] + got[e].astype(F32)

    send[0] = total(1).astype(BF)
    send[1] = total(2).astype(BF)
    rest[0] = total(0)
    rest[1] = total(3)


def second_half(rest, got, send, hold):
    hold[...] = rest[0] + got[0].astype(F32)
    send[...] = (rest[1] + got[1].astype(F32)).astype(BF)


def settle(hold, got, own, msgs):
    msgs[:TILE] = (hold[...] + got[...].astype(F32)).astype(BF)
    msgs[TILE:, : 2 * TILE] = own[...]
    msgs[TILE:, 2 * TILE :] = jnp.zeros((4 * ROWS, CHUNK - 2 * TILE), BF)


def transform(place, msgs, got, weights, send, rest, own, part):
    core = place[1]

    def times(value, i):
        block = weights[:, pl.ds(pl.multiple_of(i * ROWS, ROWS), ROWS)].reshape(PIECE, WIDE)
        return jnp.dot(value, block, preferred_element_type=F32)

    total = None
    for c, ref in ((core, msgs), (1 - core, got)):
        for z in range(4):
            spot = pl.ds(pl.multiple_of((2 * z + c) * ROWS, ROWS), ROWS)
            own[spot] = ref[TILE + z * ROWS : TILE + (z + 1) * ROWS, :PIECE]
        for i in range(2):
            value = times(ref[:TILE, i * PIECE : (i + 1) * PIECE], 2 * c + i)
            total = value if total is None else total + value
    part[...] = total + times(own[...], PARTS - 1)
    here, near, far, last = ranks(place[0], place[1])
    for i, z in enumerate((near, far, here, last)):
        rows = part[pl.ds(pl.multiple_of(z * 2 * ROWS, 2 * ROWS), 2 * ROWS)]
        if i < 2:
            send[i] = rows.astype(BF)
        else:
            rest[i - 2] = rows


def finish(place, hold, got, mine, other, total):
    value = hold[...] + got[...].astype(F32)
    total[...] = jnp.maximum(value, 0.0)
    core = place[1]
    mine[...] = total[pl.ds(pl.multiple_of(core * ROWS, ROWS), ROWS)].astype(BF)
    other[...] = total[pl.ds(pl.multiple_of((1 - core) * ROWS, ROWS), ROWS)].astype(BF)


def place_columns(place, mine, got, out):
    core = place[1]
    for c, ref in ((core, mine), (1 - core, got)):
        for z in range(4):
            spot = pl.ds(pl.multiple_of((2 * z + c) * TILE, TILE), TILE)
            out[:, spot] = ref[:, z * TILE : (z + 1) * TILE]


def exchange(x, axis):
    return lax.all_to_all(x, axis, split_axis=0, concat_axis=0, tiled=True)


def spread(x, axis):
    return exchange(jnp.broadcast_to(x, (lax.axis_size(axis), *x.shape)), axis)


def partner(x, step):
    def goal(zh, core):
        return (zh, 1 - core) if step == 0 else (ranks(zh, core)[2 * step - 1], core)

    pairs = [(2 * z + c, goal(z, c)) for z in range(4) for c in range(2)]
    return lax.ppermute(x, REL, [(i, 2 * z + c) for i, (z, c) in pairs])


def on_device(features, bases, coefficients, tile_values, tile_source, tile_relation, tile_count):
    place = jnp.stack([lax.axis_index(a) for a in REL]).astype(jnp.int32)
    padded, copies = call(
        start,
        (shape(BF, ROWS, 8 * TILE), shape(BF, 4, ROWS, DIN + PARTS * TILE)),
        [HBM] * 3,
        [
            pltpu.VMEM((ROWS, DIN), BF),
            pltpu.VMEM((RELS + 1, bases.shape[0]), F32),
            pltpu.VMEM((PER, bases.shape[0], TILE), BF),
            pltpu.VMEM((PARTS, ROWS, TILE), F32),
            pltpu.SemaphoreType.DMA((3,)),
        ],
        limit=60,
    )(features[0], coefficients, jnp.swapaxes(bases, 0, 1))
    gathered = exchange(copies, "zl")
    dense = call(
        densify,
        shape(BF, RELS + 1, TILE, SRC * TILE),
        [SMEM, SMEM, SMEM, VMEM],
        [pltpu.VMEM((RELS * SRC, TILE, TILE), F32)],
        pl.CostEstimate(flops=1 << 20, bytes_accessed=1 << 23, transcendentals=0),
    )(tile_count[0], tile_source[0, 0], tile_relation[0, 0], tile_values[0, 0])
    feats = spread(gathered[:, :, :DIN].reshape(NODES, DIN), YX).reshape(SRC * TILE, DIN)

    block = shape(BF, 2 * ROWS + 4 * QUART, TILE)
    blocks = shape(BF, 2, 2 * ROWS + 4 * QUART, TILE)
    send, mine, relay = call(sort, (blocks, block, block), [SMEM, VMEM, VMEM], [pltpu.VMEM((4, PARTS * ROWS, TILE), BF)])(
        place, padded, gathered
    )
    first = partner(send, 1)
    relay = call(pass_on, blocks, [ANY, VMEM, VMEM])(dense, relay, first)
    second = partner(relay, 2)
    own, rows = call(
        join_groups,
        (shape(BF, 4 * ROWS, 2 * TILE), shape(BF, 4 * QUART, WIDE)),
        [SMEM] + [VMEM] * 3,
    )(place, mine, first, second)

    send = call(functools.partial(aggregate, 1), shape(BF, 4, TILE, CHUNK), [SMEM, VMEM, VMEM, ANY])(
        place, dense, feats, rows
    )
    keep = call(functools.partial(aggregate, 0), shape(F32, 4, TILE, CHUNK), [SMEM, VMEM, VMEM, ANY])(
        place, dense, feats, send
    )
    two = shape(BF, 2, TILE, CHUNK)
    send, rest = call(first_half, (two, shape(F32, 2, TILE, CHUNK)), [VMEM] * 2)(keep, partner(send, 0))
    send, hold = call(
        second_half,
        (shape(BF, TILE, CHUNK), shape(F32, TILE, CHUNK)),
        [VMEM] * 2,
        cost=pl.CostEstimate(flops=WEIGHT, bytes_accessed=1 << 20, transcendentals=0),
    )(rest, partner(send, 1))
    weights = spread(rows, YX)
    msgs = call(settle, shape(BF, TILE + 4 * ROWS, CHUNK), [VMEM] * 3)(hold, partner(send, 2), own)
    pair = shape(BF, 2, 2 * ROWS, WIDE)
    send, rest = call(
        transform,
        (pair, shape(F32, 2, 2 * ROWS, WIDE)),
        [SMEM] + [VMEM] * 3,
        [pltpu.VMEM((TILE, PIECE), BF), pltpu.VMEM((TILE, WIDE), F32)],
    )(place, msgs, partner(msgs, 0), weights)
    send, hold = call(
        second_half, (shape(BF, 2 * ROWS, WIDE), shape(F32, 2 * ROWS, WIDE)), [VMEM] * 2
    )(rest, partner(send, 1))
    half = shape(BF, ROWS, WIDE)
    mine, other = call(finish, (half, half), [SMEM, VMEM, VMEM], [pltpu.VMEM((2 * ROWS, WIDE), F32)])(
        place, hold, partner(send, 2)
    )
    out = call(place_columns, shape(BF, ROWS, DOUT), [SMEM, VMEM, VMEM])(
        place, mine, partner(other, 0)
    )
    return out[None]


def solution(mesh):
    split = Mesh(mesh.devices.reshape(4, 4, 4, 4, 2), NODE + REL)
    return jax.shard_map(
        on_device,
        mesh=split,
        in_specs=(
            P(REL, NODE, None),
            P(None, NODE, REL),
            P(),
            P(NODE, REL, None, None, None),
            P(NODE, REL, None),
            P(NODE, REL, None),
            P(NODE, REL),
        ),
        out_specs=P(REL, NODE, None),
        check_vma=False,
    )
```

```python
import functools

import jax
import jax.numpy as jnp
from jax import lax
from jax.experimental import pallas as pl
from jax.experimental.pallas import tpu as pltpu
from jax.sharding import Mesh
from jax.sharding import PartitionSpec as P

BF = jnp.bfloat16
F32 = jnp.float32
NODE = ("y", "x", "zl")
REL = ("zh", "core")
YX = ("y", "x")
VMEM = pl.BlockSpec(memory_space=pltpu.VMEM)
ANY = pl.BlockSpec(memory_space=pl.ANY)
HBM = pl.BlockSpec(memory_space=pltpu.HBM)
SMEM = pl.BlockSpec(memory_space=pltpu.SMEM)

RELS = 5
DIN = 768
DOUT = 1024
TILE = 128
SRC = 8
ROWS = 16
NODES = 64
PER = 12
SLOT = 8
SELF = 2
CHUNK = SLOT * NODES
QUART = 2 * (SLOT + SELF)
PARTS = 5
WIDE = DOUT // 2
PIECE = 256
WEIGHT = 10**11


def call(body, outs, ins, scratch=(), cost=None, limit=16):
    return pl.pallas_call(
        body,
        cost_estimate=cost,
        out_shape=outs,
        in_specs=ins,
        out_specs=jax.tree.map(lambda _: VMEM, outs),
        scratch_shapes=list(scratch),
        compiler_params=pltpu.CompilerParams(vmem_limit_bytes=limit * 1024 * 1024),
    )


def shape(kind, *dims):
    return jax.ShapeDtypeStruct(dims, kind)


def start(own_in, coef_in, bases_in, padded, copies, own, coef, bases, rows, sems):
    moves = [
        pltpu.make_async_copy(src, dst, sems.at[i])
        for i, (src, dst) in enumerate(((own_in, own), (coef_in, coef), (bases_in, bases)))
    ]
    for move in moves:
        move.start()
    src = lax.broadcasted_iota(jnp.int32, (DIN, DIN), 0)
    out = lax.broadcasted_iota(jnp.int32, (DIN, DIN), 1)
    goal = PER * ((out & (PIECE - 1)) >> 2) + 4 * (out >> 8) + (out & 3)
    swap = jnp.where(src == goal, 1.0, 0.0).astype(BF)
    rows[...] = jnp.zeros_like(rows)
    for move in moves:
        move.wait()
    value = jnp.dot(own[...], swap, preferred_element_type=F32).astype(BF)
    padded[:, :DIN] = value
    padded[:, DIN:] = jnp.zeros((ROWS, 8 * TILE - DIN), BF)
    for d in range(PER):
        part = jnp.dot(
            coef[...], bases[d].astype(F32), precision=lax.Precision.HIGHEST, preferred_element_type=F32
        )
        for r in range(RELS):
            piece = 3 * r + d // 4
            spot = piece // 4 * 4 + d % 4
            rows[piece % 4, spot : spot + 1] = part[r : r + 1]
        rows[PARTS - 1, d : d + 1] = part[RELS:]
    for i in range(4):
        copies[i, :, :DIN] = value
        for k in range(PARTS):
            copies[i, :, DIN + k * TILE : DIN + (k + 1) * TILE] = rows[k].astype(BF)


def ranks(zh, core):
    one = 1 + 2 * core
    return zh, zh ^ one, zh ^ 2, zh ^ (4 - one)


def sort(place, padded, gathered, send, mine, relay, table):
    wide = gathered[:, :, DIN:].astype(F32)
    for z in range(4):
        for i in range(PARTS):
            rows = [wide[k, 4 * z : 4 * z + 4, i * TILE : (i + 1) * TILE] for k in range(4)]
            table[z, i * ROWS : (i + 1) * ROWS] = jnp.concatenate(rows, axis=0).astype(BF)
    here, near, far, last = ranks(place[0], place[1])
    for z, ref in ((near, send.at[0]), (far, send.at[1]), (here, mine), (last, relay)):
        for i in range(2):
            spot = pl.ds(pl.multiple_of(z * PIECE + i * TILE, TILE), TILE)
            ref[i * ROWS : (i + 1) * ROWS] = padded[:, spot]
        ref[2 * ROWS :] = table[z]


def pass_on(after, relay, got, send):
    send[0] = relay[...]
    send[1] = got[1]


def join_groups(place, mine, first, second, own, rows):
    here, near, far, last = ranks(place[0], place[1])
    for z, ref in ((here, mine), (near, first.at[0]), (last, second.at[0]), (far, second.at[1])):
        spot = pl.ds(pl.multiple_of(z * ROWS, ROWS), ROWS)
        own[spot, :TILE] = ref[:ROWS]
        own[spot, TILE:] = ref[ROWS : 2 * ROWS]
        rows[:, pl.ds(pl.multiple_of(z * TILE, TILE), TILE)] = ref[2 * ROWS :]


def densify(count, source, relation, values, dense, acc):
    acc[...] = jnp.zeros_like(acc)

    def add(t, _):
        spot = relation[t] * SRC + source[t]
        acc[spot] = acc[spot] + values[t].astype(F32)
        return 0

    lax.fori_loop(0, count[0], add, 0)
    for r in range(RELS):
        for s in range(SRC):
            dense[r, :, s * TILE : (s + 1) * TILE] = acc[r * SRC + s].astype(BF)


def aggregate(owner, place, dense, feats, after, out, rows, full):
    core = place[1] ^ owner
    for r in range(RELS):
        for z in range(4):
            spot = pl.ds(pl.multiple_of((2 * z + core) * ROWS, ROWS), ROWS)
            rows[(4 * r + z) * ROWS : (4 * r + z + 1) * ROWS] = dense[r, spot]
    value = jnp.dot(rows[...], feats[...], preferred_element_type=F32)
    for r in range(RELS):
        for i in range(3):
            full[3 * r + i] = value[4 * ROWS * r : 4 * ROWS * (r + 1), i * PIECE : (i + 1) * PIECE]
    full[3 * RELS] = jnp.zeros((4 * ROWS, PIECE), F32)
    for e, z in enumerate(ranks(place[0], core)):
        for i in range(4):
            out[e, :, i * PIECE : (i + 1) * PIECE] = full[4 * z + i].astype(out.dtype)


def first_half(keep, got, rows, send, rest, same):
    same[...] = rows[...]

    def total(e):
        return keep[e] + got[e].astype(F32)

    send[0] = total(1).astype(BF)
    send[1] = total(2).astype(BF)
    rest[0] = total(0)
    rest[1] = total(3)


def second_half(rest, got, send, hold):
    hold[...] = rest[0] + got[0].astype(F32)
    send[...] = (rest[1] + got[1].astype(F32)).astype(BF)


def hand(after, value, same):
    same[...] = value[...]


def transform(place, hold, got, own, weights, others, send, rest, part):
    core = place[1]
    value = (hold[...] + got[...].astype(F32)).astype(BF)
    for c, ref in ((core, weights), (1 - core, others)):
        total = None
        for i in range(PARTS):
            block = ref[:, i * ROWS : (i + 1) * ROWS].reshape(PIECE, WIDE)
            left = value[:, i * PIECE : (i + 1) * PIECE] if i < 4 else own[...]
            term = jnp.dot(left, block, preferred_element_type=F32)
            total = term if total is None else total + term
        for z in range(4):
            spot = pl.ds(pl.multiple_of((2 * z + c) * TILE, TILE), TILE)
            part[:, spot] = total[:, z * TILE : (z + 1) * TILE]
    here, near, far, last = ranks(place[0], core)
    for i, z in enumerate((near, far, here, last)):
        rows = part[pl.ds(pl.multiple_of(z * ROWS, ROWS), ROWS)]
        if i < 2:
            send[i] = rows.astype(BF)
        else:
            rest[i - 2] = rows


def finish(hold, got, out):
    out[...] = jnp.maximum(hold[...] + got[...].astype(F32), 0.0).astype(BF)


def exchange(x, axis):
    return lax.all_to_all(x, axis, split_axis=0, concat_axis=0, tiled=True)


def spread(x, axis):
    return exchange(jnp.broadcast_to(x, (lax.axis_size(axis), *x.shape)), axis)


def partner(x, step):
    def goal(zh, core):
        return (zh, 1 - core) if step == 0 else (ranks(zh, core)[2 * step - 1], core)

    pairs = [(2 * z + c, goal(z, c)) for z in range(4) for c in range(2)]
    return lax.ppermute(x, REL, [(i, 2 * z + c) for i, (z, c) in pairs])


def on_device(features, bases, coefficients, tile_values, tile_source, tile_relation, tile_count):
    place = jnp.stack([lax.axis_index(a) for a in REL]).astype(jnp.int32)
    padded, copies = call(
        start,
        (shape(BF, ROWS, 8 * TILE), shape(BF, 4, ROWS, DIN + PARTS * TILE)),
        [HBM] * 3,
        [
            pltpu.VMEM((ROWS, DIN), BF),
            pltpu.VMEM((RELS + 1, bases.shape[0]), F32),
            pltpu.VMEM((PER, bases.shape[0], TILE), BF),
            pltpu.VMEM((PARTS, ROWS, TILE), F32),
            pltpu.SemaphoreType.DMA((3,)),
        ],
        limit=60,
    )(features[0], coefficients, jnp.swapaxes(bases, 0, 1))
    gathered = exchange(copies, "zl")
    dense = call(
        densify,
        shape(BF, RELS, TILE, SRC * TILE),
        [SMEM, SMEM, SMEM, VMEM],
        [pltpu.VMEM((RELS * SRC, TILE, TILE), F32)],
        pl.CostEstimate(flops=1 << 20, bytes_accessed=1 << 23, transcendentals=0),
    )(tile_count[0], tile_source[0, 0], tile_relation[0, 0], tile_values[0, 0])
    feats = spread(gathered[:, :, :DIN].reshape(NODES, DIN), YX).reshape(SRC * TILE, DIN)

    block = shape(BF, 2 * ROWS + 4 * QUART, TILE)
    blocks = shape(BF, 2, 2 * ROWS + 4 * QUART, TILE)
    send, mine, relay = call(sort, (blocks, block, block), [SMEM, VMEM, VMEM], [pltpu.VMEM((4, PARTS * ROWS, TILE), BF)])(
        place, padded, gathered
    )
    first = partner(send, 1)
    relay = call(pass_on, blocks, [ANY, VMEM, VMEM])(dense, relay, first)
    second = partner(relay, 2)
    own, rows = call(
        join_groups,
        (shape(BF, 4 * ROWS, 2 * TILE), shape(BF, 4 * QUART, WIDE)),
        [SMEM] + [VMEM] * 3,
    )(place, mine, first, second)

    mid = (4 * ROWS, 4 * PIECE)
    scratch = [pltpu.VMEM((4 * RELS * ROWS, SRC * TILE), BF), pltpu.VMEM((16, 4 * ROWS, PIECE), F32)]
    ins = [SMEM, VMEM, VMEM, ANY]
    send = call(functools.partial(aggregate, 1), shape(BF, 4, *mid), ins, scratch)(place, dense, feats, rows)
    keep = call(functools.partial(aggregate, 0), shape(F32, 4, *mid), ins, scratch)(place, dense, feats, send)
    send, rest, rows = call(
        first_half, (shape(BF, 2, *mid), shape(F32, 2, *mid), shape(BF, 4 * QUART, WIDE)), [VMEM] * 3
    )(keep, partner(send, 0), rows)
    send, hold = call(
        second_half,
        (shape(BF, *mid), shape(F32, *mid)),
        [VMEM] * 2,
        cost=pl.CostEstimate(flops=WEIGHT, bytes_accessed=1 << 20, transcendentals=0),
    )(rest, partner(send, 1))
    got = partner(send, 2)
    weights = call(hand, shape(BF, 16, 4 * QUART, WIDE), [ANY, VMEM])(got, spread(rows, YX))
    send, rest = call(
        transform,
        (shape(BF, 2, ROWS, DOUT), shape(F32, 2, ROWS, DOUT)),
        [SMEM] + [VMEM] * 5,
        [pltpu.VMEM((4 * ROWS, DOUT), F32)],
    )(place, hold, got, own, weights, partner(weights, 0))
    send, hold = call(second_half, (shape(BF, ROWS, DOUT), shape(F32, ROWS, DOUT)), [VMEM] * 2)(
        rest, partner(send, 1)
    )
    return call(finish, shape(BF, ROWS, DOUT), [VMEM] * 2)(hold, partner(send, 2))[None]


def solution(mesh):
    split = Mesh(mesh.devices.reshape(4, 4, 4, 4, 2), NODE + REL)
    return jax.shard_map(
        on_device,
        mesh=split,
        in_specs=(
            P(REL, NODE, None),
            P(None, NODE, REL),
            P(),
            P(NODE, REL, None, None, None),
            P(NODE, REL, None),
            P(NODE, REL, None),
            P(NODE, REL),
        ),
        out_specs=P(REL, NODE, None),
        check_vma=False,
    )
```

```python
import functools

import jax
import jax.numpy as jnp
from jax import lax
from jax.experimental import pallas as pl
from jax.experimental.pallas import tpu as pltpu
from jax.sharding import Mesh
from jax.sharding import PartitionSpec as P

BF = jnp.bfloat16
F32 = jnp.float32
NODE = ("y", "x", "zl")
REL = ("zh", "core")
YX = ("y", "x")
VMEM = pl.BlockSpec(memory_space=pltpu.VMEM)
ANY = pl.BlockSpec(memory_space=pl.ANY)
HBM = pl.BlockSpec(memory_space=pltpu.HBM)
SMEM = pl.BlockSpec(memory_space=pltpu.SMEM)

RELS = 5
DIN = 768
DOUT = 1024
TILE = 128
SRC = 8
ROWS = 16
NODES = 64
PER = 12
SLOT = 8
SELF = 2
CHUNK = SLOT * NODES
QUART = 2 * (SLOT + SELF)
PARTS = 5
WIDE = DOUT // 2
PIECE = 256
WEIGHT = 10**11


def call(body, outs, ins, scratch=(), cost=None, limit=16):
    return pl.pallas_call(
        body,
        cost_estimate=cost,
        out_shape=outs,
        in_specs=ins,
        out_specs=jax.tree.map(lambda _: VMEM, outs),
        scratch_shapes=list(scratch),
        compiler_params=pltpu.CompilerParams(vmem_limit_bytes=limit * 1024 * 1024),
    )


def shape(kind, *dims):
    return jax.ShapeDtypeStruct(dims, kind)


def start(own_in, coef_in, bases_in, padded, copies, own, coef, bases, rows, sems):
    moves = [
        pltpu.make_async_copy(src, dst, sems.at[i])
        for i, (src, dst) in enumerate(((own_in, own), (coef_in, coef), (bases_in, bases)))
    ]
    for move in moves:
        move.start()
    src = lax.broadcasted_iota(jnp.int32, (DIN, DIN), 0)
    out = lax.broadcasted_iota(jnp.int32, (DIN, DIN), 1)
    goal = PER * ((out & (PIECE - 1)) >> 2) + 4 * (out >> 8) + (out & 3)
    swap = jnp.where(src == goal, 1.0, 0.0).astype(BF)
    rows[...] = jnp.zeros_like(rows)
    for move in moves:
        move.wait()
    value = jnp.dot(own[...], swap, preferred_element_type=F32).astype(BF)
    padded[:, :DIN] = value
    padded[:, DIN:] = jnp.zeros((ROWS, 8 * TILE - DIN), BF)
    for d in range(PER):
        part = jnp.dot(
            coef[...], bases[d].astype(F32), precision=lax.Precision.HIGHEST, preferred_element_type=F32
        )
        for r in range(RELS):
            piece = 3 * r + d // 4
            spot = piece // 4 * 4 + d % 4
            rows[piece % 4, spot : spot + 1] = part[r : r + 1]
        rows[PARTS - 1, d : d + 1] = part[RELS:]
    for i in range(4):
        copies[i, :, :DIN] = value
        for k in range(PARTS):
            copies[i, :, DIN + k * TILE : DIN + (k + 1) * TILE] = rows[k].astype(BF)


def ranks(zh, core):
    one = 1 + 2 * core
    return zh, zh ^ one, zh ^ 2, zh ^ (4 - one)


def sort(place, padded, gathered, send, mine, relay, table):
    wide = gathered[:, :, DIN:].astype(F32)
    for z in range(4):
        for i in range(PARTS):
            rows = [wide[k, 4 * z : 4 * z + 4, i * TILE : (i + 1) * TILE] for k in range(4)]
            table[z, i * ROWS : (i + 1) * ROWS] = jnp.concatenate(rows, axis=0).astype(BF)
    here, near, far, last = ranks(place[0], place[1])
    for z, ref in ((near, send.at[0]), (far, send.at[1]), (here, mine), (last, relay)):
        for i in range(2):
            spot = pl.ds(pl.multiple_of(z * PIECE + i * TILE, TILE), TILE)
            ref[i * ROWS : (i + 1) * ROWS] = padded[:, spot]
        ref[2 * ROWS :] = table[z]


def pass_on(after, relay, got, send):
    send[0] = relay[...]
    send[1] = got[1]


def join_groups(place, mine, first, second, own, rows):
    here, near, far, last = ranks(place[0], place[1])
    for z, ref in ((here, mine), (near, first.at[0]), (last, second.at[0]), (far, second.at[1])):
        spot = pl.ds(pl.multiple_of(z * ROWS, ROWS), ROWS)
        own[spot, :TILE] = ref[:ROWS]
        own[spot, TILE:] = ref[ROWS : 2 * ROWS]
        rows[:, pl.ds(pl.multiple_of(z * TILE, TILE), TILE)] = ref[2 * ROWS :]


def densify(count, source, relation, values, dense, acc):
    acc[...] = jnp.zeros_like(acc)

    def add(t, _):
        spot = relation[t] * SRC + source[t]
        acc[spot] = acc[spot] + values[t].astype(F32)
        return 0

    lax.fori_loop(0, count[0], add, 0)
    for r in range(RELS):
        for s in range(SRC):
            dense[r, :, s * TILE : (s + 1) * TILE] = acc[r * SRC + s].astype(BF)


def aggregate(owner, place, dense, feats, after, out, rows, full):
    core = place[1] ^ owner
    for r in range(RELS):
        for z in range(4):
            spot = pl.ds(pl.multiple_of((2 * z + core) * ROWS, ROWS), ROWS)
            rows[(4 * r + z) * ROWS : (4 * r + z + 1) * ROWS] = dense[r, spot]
    value = jnp.dot(rows[...], feats[...], preferred_element_type=F32)
    for r in range(RELS):
        for i in range(3):
            full[3 * r + i] = value[4 * ROWS * r : 4 * ROWS * (r + 1), i * PIECE : (i + 1) * PIECE]
    full[3 * RELS] = jnp.zeros((4 * ROWS, PIECE), F32)
    for e, z in enumerate(ranks(place[0], core)):
        for i in range(4):
            out[e, :, i * PIECE : (i + 1) * PIECE] = full[4 * z + i].astype(out.dtype)


def first_half(keep, got, rows, send, rest, same):
    same[...] = rows[...]

    def total(e):
        return keep[e] + got[e].astype(F32)

    send[0] = total(1).astype(BF)
    send[1] = total(2).astype(BF)
    rest[0] = total(0)
    rest[1] = total(3)


def second_half(rest, got, send, hold):
    hold[...] = rest[0] + got[0].astype(F32)
    send[...] = (rest[1] + got[1].astype(F32)).astype(BF)


def hand(after, value, same):
    same[...] = value[...]


def product(value, own, block):
    total = jnp.dot(own, block[:, 4 * ROWS :].reshape(PIECE, WIDE), preferred_element_type=F32)
    for i in range(4):
        part = block[:, i * ROWS : (i + 1) * ROWS].reshape(PIECE, WIDE)
        total = total + jnp.dot(
            value[:, i * PIECE : (i + 1) * PIECE], part, preferred_element_type=F32
        )
    return total


def transform_own(hold, got, own, weights, msgs, half):
    value = (hold[...] + got[...].astype(F32)).astype(BF)
    msgs[...] = value
    half[...] = product(value, own[...], weights)


def transform(place, msgs, own, half, others, send, rest, part):
    core = place[1]
    for c, total in ((core, half[...]), (1 - core, product(msgs[...], own[...], others))):
        for z in range(4):
            spot = pl.ds(pl.multiple_of((2 * z + c) * TILE, TILE), TILE)
            part[:, spot] = total[:, z * TILE : (z + 1) * TILE]
    here, near, far, last = ranks(place[0], core)
    for i, z in enumerate((near, far, here, last)):
        rows = part[pl.ds(pl.multiple_of(z * ROWS, ROWS), ROWS)]
        if i < 2:
            send[i] = rows.astype(BF)
        else:
            rest[i - 2] = rows


def finish(hold, got, out):
    out[...] = jnp.maximum(hold[...] + got[...].astype(F32), 0.0).astype(BF)


def exchange(x, axis):
    return lax.all_to_all(x, axis, split_axis=0, concat_axis=0, tiled=True)


def spread(x, axis):
    return exchange(jnp.broadcast_to(x, (lax.axis_size(axis), *x.shape)), axis)


def partner(x, step):
    def goal(zh, core):
        return (zh, 1 - core) if step == 0 else (ranks(zh, core)[2 * step - 1], core)

    pairs = [(2 * z + c, goal(z, c)) for z in range(4) for c in range(2)]
    return lax.ppermute(x, REL, [(i, 2 * z + c) for i, (z, c) in pairs])


def on_device(features, bases, coefficients, tile_values, tile_source, tile_relation, tile_count):
    place = jnp.stack([lax.axis_index(a) for a in REL]).astype(jnp.int32)
    padded, copies = call(
        start,
        (shape(BF, ROWS, 8 * TILE), shape(BF, 4, ROWS, DIN + PARTS * TILE)),
        [HBM] * 3,
        [
            pltpu.VMEM((ROWS, DIN), BF),
            pltpu.VMEM((RELS + 1, bases.shape[0]), F32),
            pltpu.VMEM((PER, bases.shape[0], TILE), BF),
            pltpu.VMEM((PARTS, ROWS, TILE), F32),
            pltpu.SemaphoreType.DMA((3,)),
        ],
        limit=60,
    )(features[0], coefficients, jnp.swapaxes(bases, 0, 1))
    gathered = exchange(copies, "zl")
    dense = call(
        densify,
        shape(BF, RELS, TILE, SRC * TILE),
        [SMEM, SMEM, SMEM, VMEM],
        [pltpu.VMEM((RELS * SRC, TILE, TILE), F32)],
        pl.CostEstimate(flops=1 << 20, bytes_accessed=1 << 23, transcendentals=0),
    )(tile_count[0], tile_source[0, 0], tile_relation[0, 0], tile_values[0, 0])
    feats = spread(gathered[:, :, :DIN].reshape(NODES, DIN), YX).reshape(SRC * TILE, DIN)

    block = shape(BF, 2 * ROWS + 4 * QUART, TILE)
    blocks = shape(BF, 2, 2 * ROWS + 4 * QUART, TILE)
    send, mine, relay = call(sort, (blocks, block, block), [SMEM, VMEM, VMEM], [pltpu.VMEM((4, PARTS * ROWS, TILE), BF)])(
        place, padded, gathered
    )
    first = partner(send, 1)
    relay = call(pass_on, blocks, [ANY, VMEM, VMEM])(dense, relay, first)
    second = partner(relay, 2)
    own, rows = call(
        join_groups,
        (shape(BF, 4 * ROWS, 2 * TILE), shape(BF, 4 * QUART, WIDE)),
        [SMEM] + [VMEM] * 3,
    )(place, mine, first, second)

    mid = (4 * ROWS, 4 * PIECE)
    scratch = [pltpu.VMEM((4 * RELS * ROWS, SRC * TILE), BF), pltpu.VMEM((16, 4 * ROWS, PIECE), F32)]
    ins = [SMEM, VMEM, VMEM, ANY]
    send = call(functools.partial(aggregate, 1), shape(BF, 4, *mid), ins, scratch)(place, dense, feats, rows)
    keep = call(functools.partial(aggregate, 0), shape(F32, 4, *mid), ins, scratch)(place, dense, feats, send)
    send, rest, rows = call(
        first_half, (shape(BF, 2, *mid), shape(F32, 2, *mid), shape(BF, 4 * QUART, WIDE)), [VMEM] * 3
    )(keep, partner(send, 0), rows)
    send, hold = call(
        second_half,
        (shape(BF, *mid), shape(F32, *mid)),
        [VMEM] * 2,
        cost=pl.CostEstimate(flops=WEIGHT, bytes_accessed=1 << 20, transcendentals=0),
    )(rest, partner(send, 1))
    got = partner(send, 2)
    weights = call(hand, shape(BF, 16, 4 * QUART, WIDE), [ANY, VMEM])(got, spread(rows, YX))
    others = partner(weights, 0)
    msgs, half = call(transform_own, (shape(BF, *mid), shape(F32, 4 * ROWS, WIDE)), [VMEM] * 4)(
        hold, got, own, weights
    )
    send, rest = call(
        transform,
        (shape(BF, 2, ROWS, DOUT), shape(F32, 2, ROWS, DOUT)),
        [SMEM] + [VMEM] * 4,
        [pltpu.VMEM((4 * ROWS, DOUT), F32)],
    )(place, msgs, own, half, others)
    send, hold = call(second_half, (shape(BF, ROWS, DOUT), shape(F32, ROWS, DOUT)), [VMEM] * 2)(
        rest, partner(send, 1)
    )
    return call(finish, shape(BF, ROWS, DOUT), [VMEM] * 2)(hold, partner(send, 2))[None]


def solution(mesh):
    split = Mesh(mesh.devices.reshape(4, 4, 4, 4, 2), NODE + REL)
    return jax.shard_map(
        on_device,
        mesh=split,
        in_specs=(
            P(REL, NODE, None),
            P(None, NODE, REL),
            P(),
            P(NODE, REL, None, None, None),
            P(NODE, REL, None),
            P(NODE, REL, None),
            P(NODE, REL),
        ),
        out_specs=P(REL, NODE, None),
        check_vma=False,
    )
```
